256 devices in a mesh: row: 16 (over x, y_lo, core), col: 16 (over y_hi, z).
Axes of the slice: x: 4, y: 4 (y_hi: 2, y_lo: 2; y = y_hi * 2 + y_lo), z: 8, core: 2. Of those that a mesh axis runs over, the one named last changes fastest.
Arguments:
- layer_input: bfloat16 [24576, 2048], P('col', 'row'), may hold values from -65 to 65
- grad_output: bfloat16 [24576, 8192], P('col', 'row'), may hold values from -0.41462717 to 0.41462717
- hid_state: float32 [8192], P('col'), may hold values from 2 to 40
- feat_state: float32 [2048], P('row'), may hold values from 2 to 40
Outputs:
- update: float32 [8192, 2048], P('col', 'row')
- hid_new: float32 [8192], P('col')
- feat_new: float32 [2048], P('row')
- update_rms: float32 [], replicated
The draws below stay inside these ranges and needn't reach their ends.
All inputs are finite; a program needn't handle non-finite values.
Results may differ from the reference program's by a relative error of at most 0.0003.
Values may be sent and summed in bfloat16 or wider, within the bound.
A program may use at most 128 MiB of HBM per device.

```python
import math
import jax
import jax.numpy as jnp
from jax import lax

D = 2048
HID = 8192
TOKENS = 24576


def scale_table(key, rows, cols, rise):
    first, second = jax.random.split(key)
    position = jnp.arange(cols, dtype=jnp.float32) / cols
    rough = jnp.exp(jax.random.uniform(first, (cols,), jnp.float32, -0.6931472, 0.6931472))
    column_scale = rise ** position * rough
    row_scale = jnp.exp(jax.random.uniform(second, (rows, 1), jnp.float32, -0.7, 0.7))
    return row_scale * column_scale[None, :]


def token_weights(key):
    shared = jax.random.fold_in(key, 5)
    strength = float(TOKENS) ** (-0.25)
    return jax.random.truncated_normal(shared, -3.0, 3.0, (TOKENS, 2), jnp.float32) * strength


def coherent_part(weights, key, cols, spread):
    directions = jax.random.truncated_normal(key, -3.0, 3.0, (2, cols), jnp.float32) * spread
    return weights[:, 0:1] * directions[0][None, :] + weights[:, 1:2] * directions[1][None, :]


def draw_layer_input(key, part):
    weights = token_weights(key)
    key = jax.random.fold_in(key, 11)
    first, second, third = jax.random.split(key, 3)
    base = jax.random.truncated_normal(first, -4.0, 4.0, (TOKENS, D), jnp.float32)
    table = scale_table(second, TOKENS, D, 4.0)
    shared = coherent_part(weights, third, D, 2.5)
    values = jnp.clip(base * table + shared, -64.0, 64.0)
    return values.astype(jnp.bfloat16)


def draw_grad_output(key, part):
    weights = token_weights(key)
    key = jax.random.fold_in(key, 23)
    first, second, third = jax.random.split(key, 3)
    factor = float(TOKENS) ** (-0.5)
    base = jax.random.truncated_normal(first, -4.0, 4.0, (TOKENS, HID), jnp.float32)
    table = scale_table(second, TOKENS, HID, 4.0)
    shared = coherent_part(weights, third, HID, 2.5)
    values = jnp.clip(base * table + shared, -64.0, 64.0) * factor
    return values.astype(jnp.bfloat16)


def steps_of(own_key, shape, pieces, least, largest):
    factor_of, own = 1.0, jax.random.fold_in(own_key, 6)
    for dim, blocks in pieces:
        draws = jnp.exp(jax.random.uniform(jax.random.fold_in(own, dim), (blocks,), jnp.float32, least / len(pieces), largest / len(pieces)))
        factor_of = factor_of * jnp.repeat(draws, shape[dim] // blocks).reshape([-1 if axis == dim else 1 for axis in range(len(shape))])
    return factor_of


def setup_inputs(seed: int = 0) -> dict:
    keys = jax.random.split(jax.random.key(seed), 5)
    layer_input = draw_layer_input(jax.random.fold_in(keys[4], 71), 0)
    grad_output = draw_grad_output(jax.random.fold_in(keys[4], 71), 0)
    hid_state = jnp.clip(jnp.exp(math.log(40.0) - 2.9957323 * jax.random.uniform(keys[2], (HID,), jnp.float32) ** steps_of(keys[2], (HID,), ((0, 16),), -0.2, 0.2)), 2.0, 40.0)
    feat_state = jnp.clip(jnp.exp(math.log(40.0) - 2.9957323 * jax.random.uniform(keys[3], (D,), jnp.float32) ** steps_of(keys[3], (D,), ((0, 16),), -0.2, 0.2)), 2.0, 40.0)
    return {"layer_input": layer_input, "grad_output": grad_output, "hid_state": hid_state, "feat_state": feat_state}


decay_rate = 0.8415106807538887

def reference(layer_input, grad_output, hid_state, feat_state):
    block_rows = min(TOKENS, 2048)
    steps_count = TOKENS // block_rows
    inputs_blocks = layer_input.reshape(steps_count, block_rows, D)
    output_blocks = grad_output.reshape(steps_count, block_rows, HID)

    def accumulate(total, pair):
        left = pair[1].astype(jnp.float32)
        right = pair[0].astype(jnp.float32)
        term = lax.dot_general(left, right, (((0,), (0,)), ((), ())), precision=lax.Precision.HIGHEST, preferred_element_type=jnp.float32)
        return (total + term, None)
    grad, _ = lax.scan(accumulate, jnp.zeros((HID, D), jnp.float32), (inputs_blocks, output_blocks))
    squares = grad * grad + 1e-30
    hid_new = decay_rate * hid_state + (1.0 - decay_rate) * lax.optimization_barrier(jnp.mean(squares, axis=1))
    feat_new = decay_rate * feat_state + (1.0 - decay_rate) * lax.optimization_barrier(jnp.mean(squares, axis=0))
    hid_mean = jnp.mean(hid_new)
    raw = grad * jnp.sqrt(hid_mean / (hid_new[:, None] * feat_new[None, :]))
    update_rms = jnp.sqrt(jnp.mean(raw * raw))
    update = raw / jnp.maximum(1.0, update_rms)
    return (update, hid_new, feat_new, update_rms)
```

```python
import functools
import jax
import jax.numpy as jnp
from jax import lax
from jax.sharding import PartitionSpec as P
from jax.experimental import pallas as pl
from jax.experimental.pallas import tpu as pltpu

decay_rate = 0.8415106807538887
MESH = pl.DeviceIdType.MESH
PAIRS = 8
MSG = jnp.float32


def rem(a, n):
    return lax.rem(a, n)


def kernel(
    tokens, hid_count, feat_count,
    x_hbm, g_hbm, hs_ref, fs_ref,
    upd_ref, hid_ref, feat_ref, rms_ref,
    gv, gt, xp, pb, sb, rb, fin, yr, ga, ar, tile, racc, hsend, hr, hb, cs, cr, ts, tr,
    lsem, gsend, grecv, crecv, ssem, rsem, ysend, yrecv, asend, arecv, bsend, brecv,
    hsem, hrecv, hbsend, hbrecv, csend, csrecv, tsend, trecv,
):
    r = lax.axis_index("row")
    c = lax.axis_index("col")
    x, yl, k = r // 4, rem(r // 2, 2), rem(r, 2)
    yh, z = c // 8, rem(c, 8)
    part = 2 * z + yh

    def row_of(dx, dy, kk):
        return rem(x + dx, 4) * 4 + rem(yl + dy, 2) * 2 + kk

    def remote(src, dst, send, recv, dev):
        return pltpu.make_async_remote_copy(
            src_ref=src, dst_ref=dst, send_sem=send, recv_sem=recv,
            device_id=dev, device_id_type=MESH,
        )

    lanes = pl.ds(pl.multiple_of(k * 128, 128), 128)
    other_lanes = pl.ds(pl.multiple_of((1 - k) * 128, 128), 128)
    copy_x = pltpu.make_async_copy(x_hbm, xp.at[0, :, lanes], lsem.at[0])
    copy_x.start()
    copy_g = pltpu.make_async_copy(g_hbm, gv, lsem.at[1])
    copy_g.start()

    barrier = pltpu.get_barrier_semaphore()
    for i in range(1, 16):
        pl.semaphore_signal(barrier, inc=1, device_id=(rem(r + i, 16), c), device_id_type=MESH)
        pl.semaphore_signal(barrier, inc=1, device_id=(r, rem(c + i, 16)), device_id_type=MESH)
    copy_x.wait()
    pl.semaphore_wait(barrier, 30)

    east = (row_of(1, 0, k), c)
    west = (row_of(3, 0, k), c)
    side = (row_of(0, 1, k), c)
    mate = (row_of(0, 0, 1 - k), c)
    half = tokens // 2
    whole, low, high = pl.ds(0, tokens), pl.ds(0, half), pl.ds(half, half)

    def send_block(src_slot, dst_slot, rows, send, recv, dev):
        return remote(xp.at[src_slot, rows, lanes], xp.at[dst_slot, rows, lanes], gsend.at[send], grecv.at[recv], dev)

    def mate_copy(slot):
        return remote(xp.at[slot, :, lanes], xp.at[slot, :, lanes], gsend.at[8 + slot], crecv.at[slot], mate)

    sends = {
        "e0": send_block(0, 3, whole, 0, 3, east),
        "w0": send_block(0, 2, whole, 1, 2, west),
        "s0": send_block(0, 1, whole, 2, 1, side),
        "e1": send_block(1, 6, whole, 3, 6, east),
        "w1": send_block(1, 5, whole, 4, 5, west),
        "e3": send_block(3, 4, low, 5, 4, east),
        "w2": send_block(2, 4, high, 6, 0, west),
        "s4": send_block(4, 7, whole, 7, 7, side),
    }

    def wait_block(slot):
        if slot == 4:
            send_block(4, 4, low, 0, 4, east).wait_recv()
            send_block(4, 4, high, 0, 0, east).wait_recv()
        else:
            send_block(slot, slot, whole, 0, slot, east).wait_recv()

    def wait_mate(slot):
        remote(xp.at[slot, :, other_lanes], xp.at[slot, :, other_lanes], gsend.at[0], crecv.at[slot], mate).wait_recv()

    for name in ("e0", "w0", "s0"):
        sends[name].start()
    mate_copy(0).start()
    copy_g.wait()
    gt[...] = gv[...].T
    racc[...] = jnp.zeros_like(racc)

    def message(s, m, sign):
        dev = (r, yh * 8 + rem(z + sign + 8, 8))
        return remote(sb.at[s, m], rb.at[s, m], ssem.at[s, m], rsem.at[s, m], dev)

    def chunk(s, offset):
        rows = pl.ds(pl.multiple_of(rem(z + offset + 8, 8) * 64, 64), 64)
        return pb[s, rows, :]

    def index(d, sign):
        return 0 if d == 4 else 7 - 2 * d + (0 if sign > 0 else 1)

    def push(s, m, sign, value):
        sb[s, m] = value.astype(MSG)
        message(s, m, sign).start()

    def got(s, m):
        message(s, m, 1).wait_recv()
        return rb[s, m].astype(jnp.float32)

    def slot_offset(p):
        dy = jnp.where(jnp.logical_or(p == 1, p >= 5), 1, 0)
        one = jnp.logical_or(p == 2, p == 5)
        three = jnp.logical_or(p == 3, p == 6)
        two = jnp.logical_or(p == 4, p == 7)
        dx = jnp.where(one, 1, 0) + jnp.where(two, 2, 0) + jnp.where(three, 3, 0)
        return dx, dy

    y_mate = (r, (1 - yh) * 8 + z)

    def y_copy(s):
        rows = pl.ds(pl.multiple_of((1 - yh) * 32, 32), 32)
        return remote(fin.at[s, rows], yr.at[s], ysend.at[s], yrecv.at[s], y_mate)

    def a_copy(s, kk, f):
        return remote(ga.at[s, kk], ar.at[r], asend.at[s, kk], arecv.at[r], (f, c))

    def within(s):
        return jnp.logical_and(s >= 0, s < PAIRS)

    def step(t, carry):
        for d in (1, 2):
            s = t - 4 + d

            @pl.when(within(s))
            def _():
                for sign in (1, -1):
                    push(s, index(d, sign), sign, chunk(s, sign * d) + got(s, index(d + 1, sign)))

        s3 = t - 1

        @pl.when(within(s3))
        def _():
            par = rem(s3, 2)
            for sign in (1, -1):
                long = par == (0 if sign > 0 else 1)

                @pl.when(long)
                def _():
                    push(s3, index(3, sign), sign, chunk(s3, sign * 3) + got(s3, 0))

                @pl.when(jnp.logical_not(long))
                def _():
                    push(s3, index(3, sign), sign, chunk(s3, sign * 3))

        @pl.when(t == 1)
        def _():
            wait_block(1)
            mate_copy(1).start()
            wait_block(3)
            sends["e3"].start()
            mate_copy(3).start()
            wait_block(2)
            sends["w2"].start()
            mate_copy(2).start()
            sends["e1"].start()
            sends["w1"].start()

        @pl.when(t == 3)
        def _():
            wait_block(4)
            sends["s4"].start()
            mate_copy(4).start()

        for slot in (5, 6, 7):
            @pl.when(t == slot)
            def _():
                wait_block(slot)
                mate_copy(slot).start()

        @pl.when(t < PAIRS)
        def _():
            wait_mate_dyn(t)
            pb[t] = jnp.dot(gt[...], xp[t], preferred_element_type=jnp.float32)
            sign = 1 - 2 * rem(t, 2)
            push(t, 0, sign, chunk(t, 4))

        s0 = t - 4

        @pl.when(within(s0))
        def _():
            fin[s0] = chunk(s0, 0) + got(s0, 5) + got(s0, 6)
            y_copy(s0).start()

        sy = t - 5

        @pl.when(within(sy))
        def _():
            y_copy(sy).wait_recv()
            rows = pl.ds(pl.multiple_of(yh * 32, 32), 32)
            g = fin[sy, rows, :] + yr[sy]
            racc[...] += g * g + 1e-30
            dx, dy = slot_offset(sy)
            for kk in (0, 1):
                ga[sy, kk] = g[:, kk * 128:(kk + 1) * 128]
                f = row_of(dx, dy, kk)
                here = jnp.logical_and(sy == 0, k == kk)

                @pl.when(here)
                def _():
                    ar[r] = g[:, kk * 128:(kk + 1) * 128]

                @pl.when(jnp.logical_not(here))
                def _():
                    a_copy(sy, kk, f).start()

        return carry

    def wait_mate_dyn(t):
        remote(xp.at[t, :, other_lanes], xp.at[t, :, other_lanes], gsend.at[0], crecv.at[t], mate).wait_recv()

    lax.fori_loop(0, PAIRS + 5, step, 0)

    sums = jnp.sum(racc[...], axis=1, keepdims=True)
    lane = lax.broadcasted_iota(jnp.int32, (32, 128), 1)
    line = lax.broadcasted_iota(jnp.int32, (32, 128), 0)
    placed = jnp.sum(jnp.where(lane == line + rem(part, 4) * 32, sums, 0.0), axis=0, keepdims=True)
    diagonal = r == c
    h_copy = remote(hsend, hr.at[part], hsem, hrecv.at[part], (r, r))

    @pl.when(diagonal)
    def _():
        hr[part] = placed

    @pl.when(jnp.logical_not(diagonal))
    def _():
        hsend[...] = placed
        h_copy.start()

    def b_copy(q):
        return remote(ar.at[q], tile.at[part], bsend.at[q], brecv.at[part], (r, q))

    def wait_a(q):
        remote(ar.at[q], ar.at[q], asend.at[0, 0], arecv.at[q], mate).wait_recv()

    def b_step(i, carry):
        q = rem(c + i, 16)

        @pl.when(q != r)
        def _():
            wait_a(q)

        @pl.when(i == 0)
        def _():
            tile[part] = ar[c]

        @pl.when(i > 0)
        def _():
            b_copy(q).start()

        return carry

    lax.fori_loop(0, 16, b_step, 0)

    def hb_copy(i):
        return remote(hb, hb, hbsend.at[i], hbrecv, (rem(r + i, 16), c))

    @pl.when(diagonal)
    def _():
        def wait_h(i, carry):
            q = rem(part + i, 16)
            remote(hr.at[q], hr.at[q], hsem, hrecv.at[q], mate).wait_recv()
            return carry

        lax.fori_loop(1, 16, wait_h, 0)
        for q in range(4):
            total = hr[4 * q] + hr[4 * q + 1] + hr[4 * q + 2] + hr[4 * q + 3]
            hb[q:q + 1, :] = decay_rate * hs_ref[q:q + 1, :] + (1.0 - decay_rate) * (total / feat_count)

        for i in range(1, 16):
            hb_copy(i).start()

    @pl.when(jnp.logical_not(diagonal))
    def _():
        hb_copy(1).wait_recv()

    hid_ref[...] = hb[...]
    eye = lax.broadcasted_iota(jnp.int32, (128, 128), 0) == lax.broadcasted_iota(jnp.int32, (128, 128), 1)
    columns = [jnp.sum(jnp.where(eye, hb[q:q + 1, :], 0.0), axis=1, keepdims=True) for q in range(4)]

    def wait_b(i, carry):
        q = rem(part + i, 16)
        remote(tile.at[q], tile.at[q], bsend.at[0], brecv.at[q], mate).wait_recv()
        return carry

    lax.fori_loop(1, 16, wait_b, 0)
    fsum = jnp.zeros((1, 128), jnp.float32)
    wsum = jnp.zeros((1, 128), jnp.float32)
    for q in range(4):
        g = tile[4 * q:4 * q + 4].reshape(128, 128)
        sq = g * g
        fsum += jnp.sum(sq + 1e-30, axis=0, keepdims=True)
        wsum += jnp.sum(sq / columns[q], axis=0, keepdims=True)
    cr[c, 0:1, :] = fsum
    cr[c, 1:2, :] = wsum
    cr[c, 2:3, :] = jnp.full((1, 128), jnp.sum(hb[...]), jnp.float32)
    cr[c, 3:8, :] = jnp.zeros((5, 128), jnp.float32)

    def c_copy(i):
        return remote(cr.at[c], cr.at[c], csend.at[i], csrecv.at[c], (r, rem(c + i, 16)))

    for i in range(1, 16):
        c_copy(i).start()

    def wait_c(i, carry):
        q = rem(c + i, 16)
        remote(cr.at[q], cr.at[q], csend.at[0], csrecv.at[q], mate).wait_recv()
        return carry

    lax.fori_loop(1, 16, wait_c, 0)
    both = jnp.sum(cr[...], axis=0)
    feat = decay_rate * fs_ref[...] + (1.0 - decay_rate) * (both[0:1, :] / hid_count)
    feat_ref[...] = feat
    hid_mean = both[2:3, :] / hid_count
    tr[r] = jnp.full((1, 128), jnp.sum(both[1:2, :] / feat), jnp.float32)

    def t_copy(i):
        return remote(tr.at[r], tr.at[r], tsend.at[i], trecv.at[r], (rem(r + i, 16), c))

    for i in range(1, 16):
        t_copy(i).start()

    def drain(s, carry):
        for m in range(7):
            message(s, m, 1).wait_send()
        y_copy(s).wait_send()
        for kk in (0, 1):
            @pl.when(jnp.logical_not(jnp.logical_and(s == 0, k == kk)))
            def _():
                a_copy(s, kk, r).wait_send()
        mate_copy(s).wait_send()
        return carry

    lax.fori_loop(0, PAIRS, drain, 0)
    for one in sends.values():
        one.wait_send()

    def drain_b(i, carry):
        b_copy(rem(c + i, 16)).wait_send()
        c_copy(i).wait_send()
        return carry

    lax.fori_loop(1, 16, drain_b, 0)

    @pl.when(jnp.logical_not(diagonal))
    def _():
        h_copy.wait_send()

    @pl.when(diagonal)
    def _():
        for i in range(1, 16):
            hb_copy(i).wait_send()

    def wait_t(i, carry):
        q = rem(r + i, 16)
        remote(tr.at[q], tr.at[q], tsend.at[0], trecv.at[q], mate).wait_recv()
        t_copy(i).wait_send()
        return carry

    lax.fori_loop(1, 16, wait_t, 0)
    mean = hid_mean * jnp.sum(tr[...], axis=0) / (hid_count * feat_count)
    rms = jnp.sqrt(mean)
    rms_ref[...] = rms
    across = jnp.sqrt(hid_mean / feat) / jnp.maximum(1.0, rms)
    for q in range(4):
        g = tile[4 * q:4 * q + 4].reshape(128, 128)
        upd_ref[128 * q:128 * q + 128, :] = g * lax.rsqrt(columns[q]) * across


def body(layer_input, grad_output, hid_state, feat_state):
    tokens = layer_input.shape[0]
    hid_count, feat_count = 8192.0, 2048.0
    vm = pl.BlockSpec(memory_space=pltpu.VMEM)
    hbm = pl.BlockSpec(memory_space=pl.ANY)
    f32, bf16 = jnp.float32, jnp.bfloat16
    dma = pltpu.SemaphoreType.DMA
    update, hid, feat, rms = pl.pallas_call(
        functools.partial(kernel, tokens, hid_count, feat_count),
        name="optimizer_step",
        out_shape=(
            jax.ShapeDtypeStruct((512, 128), f32),
            jax.ShapeDtypeStruct((4, 128), f32),
            jax.ShapeDtypeStruct((1, 128), f32),
            jax.ShapeDtypeStruct((1, 128), f32),
        ),
        in_specs=[hbm, hbm, vm, vm],
        out_specs=(vm, vm, vm, vm),
        scratch_shapes=[
            pltpu.VMEM((tokens, 512), bf16),
            pltpu.VMEM((512, tokens), bf16),
            pltpu.VMEM((PAIRS, tokens, 256), bf16),
            pltpu.VMEM((PAIRS, 512, 256), f32),
            pltpu.VMEM((PAIRS, 7, 64, 256), MSG),
            pltpu.VMEM((PAIRS, 7, 64, 256), MSG),
            pltpu.VMEM((PAIRS, 64, 256), f32),
            pltpu.VMEM((PAIRS, 32, 256), f32),
            pltpu.VMEM((PAIRS, 2, 32, 128), f32),
            pltpu.VMEM((16, 32, 128), f32),
            pltpu.VMEM((16, 32, 128), f32),
            pltpu.VMEM((32, 256), f32),
            pltpu.VMEM((1, 128), f32),
            pltpu.VMEM((16, 1, 128), f32),
            pltpu.VMEM((4, 128), f32),
            pltpu.VMEM((8, 128), f32),
            pltpu.VMEM((16, 8, 128), f32),
            pltpu.VMEM((1, 128), f32),
            pltpu.VMEM((16, 1, 128), f32),
            dma((2,)), dma((16,)), dma((8,)), dma((PAIRS,)),
            dma((PAIRS, 7)), dma((PAIRS, 7)), dma((PAIRS,)), dma((PAIRS,)),
            dma((PAIRS, 2)), dma((16,)), dma((16,)), dma((16,)),
            dma, dma((16,)), dma((16,)), dma,
            dma((16,)), dma((16,)), dma((16,)), dma((16,)),
        ],
        compiler_params=pltpu.CompilerParams(
            collective_id=0, has_side_effects=True, vmem_limit_bytes=50 << 20
        ),
    )(layer_input, grad_output, hid_state.reshape(4, 128), feat_state.reshape(1, 128))
    return update, hid.reshape(512), feat.reshape(128), rms[0, 0]


def solution(mesh):
    in_specs = (P("col", "row"), P("col", "row"), P("col"), P("row"))
    out_specs = (P("col", "row"), P("col"), P("row"), P())
    return jax.shard_map(body, mesh=mesh, in_specs=in_specs, out_specs=out_specs, check_vma=False)
```

```python
import functools
import jax
import jax.numpy as jnp
from jax import lax
from jax.sharding import PartitionSpec as P
from jax.experimental import pallas as pl
from jax.experimental.pallas import tpu as pltpu

decay_rate = 0.8415106807538887
MESH = pl.DeviceIdType.MESH
PAIRS = 8
STEPS = 2 * PAIRS
MSG = jnp.bfloat16
POWER = 13
LIFT = 2.0 ** 9
TILE = 144
SPANS = ((2, 3, 2 * TILE, TILE), (4, 5, TILE, 2 * TILE), (6, 9, 0, 3 * TILE), (10, 11, 0, 2 * TILE), (12, 13, 0, TILE))


def rem(a, n):
    return lax.rem(a, n)


def encode(value):
    top = jnp.maximum(jnp.max(jnp.abs(value), axis=0, keepdims=True), 1e-30)
    scale = top.astype(MSG).astype(jnp.float32)
    m = value * (LIFT / scale)
    m2 = m * m
    m4 = m2 * m2
    coded = ((m * m4) * (m4 * m4)).astype(MSG)
    scales = [jnp.broadcast_to(scale[:, 128 * q:128 * q + 128], (8, 128)) for q in (0, 1)]
    return jnp.concatenate([coded[:, 0:128], coded[:, 128:256], jnp.concatenate(scales, axis=0).astype(MSG)], axis=0)


def decode(tile):
    scales = tile[128:144].astype(jnp.float32)
    parts = []
    for q in (0, 1):
        w = tile[64 * q:64 * q + 64].astype(jnp.float32)
        size = jnp.exp(jnp.log(jnp.maximum(jnp.abs(w), 1.2e-38)) * (1.0 / POWER))
        parts.append(jnp.where(w < 0.0, -size, size) * (scales[8 * q:8 * q + 1] * (1.0 / LIFT)))
    return jnp.concatenate(parts, axis=1)


def kernel(
    tokens, hid_count, feat_count,
    x_hbm, g_hbm, hs_hbm, fs_hbm,
    upd_ref, hid_ref, feat_ref, rms_ref,
    hs, hx, fs, gv, gt, xp, pb, sb4, rb4, sb, rb, fin, yr, ga, pm, ar, tile, racc, cr, tr,
    lsem, gsend, grecv, crecv, ssem4, rsem4, ssem, rsem, ysend, yrecv, asend, arecv, bsend, brecv,
    hsem, psend, precv, csend, csrecv, tsend, trecv,
):
    r = lax.axis_index("row")
    c = lax.axis_index("col")
    x, yl, k = r // 4, rem(r // 2, 2), rem(r, 2)
    yh, z = c // 8, rem(c, 8)
    part = 2 * z + yh

    def row_of(dx, dy, kk):
        return rem(x + dx, 4) * 4 + rem(yl + dy, 2) * 2 + kk

    def remote(src, dst, send, recv, dev):
        return pltpu.make_async_remote_copy(
            src_ref=src, dst_ref=dst, send_sem=send, recv_sem=recv,
            device_id=dev, device_id_type=MESH,
        )

    copy_x = pltpu.make_async_copy(x_hbm, xp.at[0, k], lsem.at[0])
    copy_x.start()
    copy_g = pltpu.make_async_copy(g_hbm, gv, lsem.at[1])
    copy_g.start()
    copy_hs = pltpu.make_async_copy(hs_hbm, hs, lsem.at[2])
    copy_hs.start()
    copy_fs = pltpu.make_async_copy(fs_hbm, fs, lsem.at[3])
    copy_fs.start()

    barrier = pltpu.get_barrier_semaphore()
    diagonal = r == c
    for i in range(1, 16):
        pl.semaphore_signal(barrier, inc=1, device_id=(rem(r + i, 16), c), device_id_type=MESH)
        pl.semaphore_signal(barrier, inc=1, device_id=(r, rem(c + i, 16)), device_id_type=MESH)

    @pl.when(jnp.logical_not(diagonal))
    def _():
        pl.semaphore_signal(barrier, inc=1, device_id=(c, r), device_id_type=MESH)

    copy_x.wait()
    pl.semaphore_wait(barrier, jnp.where(diagonal, 30, 31))

    east = (row_of(1, 0, k), c)
    west = (row_of(3, 0, k), c)
    side = (row_of(0, 1, k), c)
    mate = (row_of(0, 0, 1 - k), c)
    half = tokens // 2
    whole, low, high = pl.ds(0, tokens), pl.ds(0, half), pl.ds(half, half)

    def send_block(src_slot, dst_slot, rows, send, recv, dev):
        return remote(xp.at[src_slot, k, rows], xp.at[dst_slot, k, rows], gsend.at[send], grecv.at[recv], dev)

    def mate_copy(slot):
        return remote(xp.at[slot, k], xp.at[slot, k], gsend.at[8 + slot], crecv.at[slot], mate)

    sends = {
        "e0": send_block(0, 3, whole, 0, 3, east),
        "w0": send_block(0, 2, whole, 1, 2, west),
        "s0": send_block(0, 1, whole, 2, 1, side),
        "e1": send_block(1, 6, whole, 3, 6, east),
        "w1": send_block(1, 5, whole, 4, 5, west),
        "e3": send_block(3, 4, low, 5, 4, east),
        "w2": send_block(2, 4, high, 6, 0, west),
        "s4": send_block(4, 7, whole, 7, 7, side),
    }

    def wait_block(slot):
        if slot == 4:
            send_block(4, 4, low, 0, 4, east).wait_recv()
            send_block(4, 4, high, 0, 0, east).wait_recv()
        else:
            send_block(slot, slot, whole, 0, slot, east).wait_recv()

    def wait_mate(slot):
        remote(xp.at[slot, 1 - k], xp.at[slot, 1 - k], gsend.at[0], crecv.at[slot], mate).wait_recv()

    for name in ("e0", "w0", "s0"):
        sends[name].start()
    mate_copy(0).start()

    far = 2 * rem(r, 8) + r // 8
    copy_hs.wait()
    hx_copy = remote(hs.at[far // 4], hx, hsem.at[0], hsem.at[1], (c, r))

    @pl.when(diagonal)
    def _():
        hx[...] = hs[part // 4]

    @pl.when(jnp.logical_not(diagonal))
    def _():
        hx_copy.start()

    copy_g.wait()
    copy_fs.wait()
    gt[...] = gv[...].T
    racc[...] = jnp.zeros_like(racc)

    def z_dev(sign):
        return (r, yh * 8 + rem(z + sign + 8, 8))

    def first_copy(s, sign):
        return remote(sb4.at[s], rb4.at[s], ssem4.at[s], rsem4.at[s], z_dev(sign))

    def span_copy(t, way, first, rows):
        at = pl.ds(first, rows)
        return remote(sb.at[t, way, at], rb.at[t, way, at], ssem.at[t, way], rsem.at[t, way], z_dev(1 - 2 * way))

    def spans(t, act):
        for begin, end, first, rows in SPANS:
            @pl.when(jnp.logical_and(t >= begin, t <= end))
            def _():
                for way in (0, 1):
                    act(span_copy(t, way, first, rows))

    def chunk(s, offset):
        rows = pl.ds(pl.multiple_of(rem(z + offset + 8, 8) * 64, 64), 64)
        return pb[s, rows, :]

    def put(t, way, d, value):
        sb[t, way, TILE * (d - 1):TILE * d] = encode(value)

    def got(t, way, d):
        return decode(rb[t, way, TILE * (d - 1):TILE * d])

    def slot_offset(p):
        dy = jnp.where(jnp.logical_or(p == 1, p >= 5), 1, 0)
        one = jnp.logical_or(p == 2, p == 5)
        three = jnp.logical_or(p == 3, p == 6)
        two = jnp.logical_or(p == 4, p == 7)
        dx = jnp.where(one, 1, 0) + jnp.where(two, 2, 0) + jnp.where(three, 3, 0)
        return dx, dy

    y_mate = (r, (1 - yh) * 8 + z)

    def y_copy(s):
        rows = pl.ds(pl.multiple_of((1 - yh) * 32, 32), 32)
        return remote(fin.at[s, rows], yr.at[s], ysend.at[s], yrecv.at[s], y_mate)

    def a_copy(s, kk, f):
        return remote(ga.at[s, kk], ar.at[r, 0:32], asend.at[s, kk], arecv.at[r], (f, c))

    def p_copy(s, kk, f):
        return remote(pm.at[s, kk], ar.at[r, 32:40], psend.at[s, kk], precv.at[r], (f, c))

    def mine(s, kk):
        return jnp.logical_and(s == 0, k == kk)

    def within(s):
        return jnp.logical_and(s >= 0, s < PAIRS)

    def step(t, carry):
        spans(t - 2, lambda copy: copy.wait_recv())
        s0 = t - 8

        @pl.when(within(s0))
        def _():
            fin[s0] = chunk(s0, 0) + got(t - 2, 0, 1) + got(t - 2, 1, 1)
            y_copy(s0).start()

        for d in (1, 2):
            s = t - 8 + 2 * d

            @pl.when(within(s))
            def _():
                for way in (0, 1):
                    put(t, way, d, chunk(s, (1 - 2 * way) * d) + got(t - 2, way, d + 1))

        s3 = t - 2

        @pl.when(within(s3))
        def _():
            first_copy(s3, 1).wait_recv()
            for way in (0, 1):
                long = rem(s3, 2) == way

                @pl.when(long)
                def _():
                    put(t, way, 3, chunk(s3, (1 - 2 * way) * 3) + decode(rb4[s3]))

                @pl.when(jnp.logical_not(long))
                def _():
                    put(t, way, 3, chunk(s3, (1 - 2 * way) * 3))

        spans(t, lambda copy: copy.start())

        @pl.when(t == 1)
        def _():
            wait_block(1)
            mate_copy(1).start()
            wait_block(3)
            sends["e3"].start()
            mate_copy(3).start()
            wait_block(2)
            sends["w2"].start()
            mate_copy(2).start()
            sends["e1"].start()
            sends["w1"].start()

        @pl.when(t == 3)
        def _():
            wait_block(4)
            sends["s4"].start()
            mate_copy(4).start()

        for slot in (5, 6, 7):
            @pl.when(t == slot)
            def _():
                wait_block(slot)
                mate_copy(slot).start()

        @pl.when(t < PAIRS)
        def _():
            wait_mate(t)
            both = jnp.concatenate([xp[t, 0], xp[t, 1]], axis=1)
            pb[t] = jnp.dot(gt[...], both, preferred_element_type=jnp.float32)
            sb4[t] = encode(chunk(t, 4))
            first_copy(t, 1 - 2 * rem(t, 2)).start()

        sy = t - 9

        @pl.when(within(sy))
        def _():
            y_copy(sy).wait_recv()
            rows = pl.ds(pl.multiple_of(yh * 32, 32), 32)
            g = fin[sy, rows, :] + yr[sy]
            racc[...] += g * g + 1e-30
            dx, dy = slot_offset(sy)
            for kk in (0, 1):
                ga[sy, kk] = g[:, kk * 128:(kk + 1) * 128]

                @pl.when(mine(sy, kk))
                def _():
                    ar[r, 0:32] = g[:, kk * 128:(kk + 1) * 128]

                @pl.when(jnp.logical_not(mine(sy, kk)))
                def _():
                    a_copy(sy, kk, row_of(dx, dy, kk)).start()

        return carry

    lax.fori_loop(0, STEPS + 1, step, 0)

    @pl.when(jnp.logical_not(diagonal))
    def _():
        hx_copy.wait_recv()

    sums = jnp.sum(racc[...], axis=1, keepdims=True)
    lane = lax.broadcasted_iota(jnp.int32, (32, 128), 1)
    line = lax.broadcasted_iota(jnp.int32, (32, 128), 0)
    place = lane == line + rem(part, 4) * 32
    old = jnp.sum(jnp.where(place, hx[...], 0.0), axis=1, keepdims=True)
    hid = decay_rate * old + (1.0 - decay_rate) * (sums / feat_count)
    hid_row = jnp.sum(jnp.where(place, hid, 0.0), axis=0, keepdims=True)
    hid_sum = jnp.full((1, 128), jnp.sum(hid), jnp.float32)
    inverse = 1.0 / hid

    def p_step(s, carry):
        dx, dy = slot_offset(s)
        for kk in (0, 1):
            sq = ga[s, kk] * ga[s, kk]
            pm[s, kk, 0:1] = hid_row
            pm[s, kk, 1:2] = jnp.sum(sq + 1e-30, axis=0, keepdims=True)
            pm[s, kk, 2:3] = jnp.sum(sq * inverse, axis=0, keepdims=True)
            pm[s, kk, 3:4] = hid_sum
            pm[s, kk, 4:8] = jnp.zeros((4, 128), jnp.float32)

            @pl.when(mine(s, kk))
            def _():
                ar[r, 32:40] = pm[s, kk]

            @pl.when(jnp.logical_not(mine(s, kk)))
            def _():
                p_copy(s, kk, row_of(dx, dy, kk)).start()

        return carry

    lax.fori_loop(0, PAIRS, p_step, 0)

    def wait_p(i, carry):
        q = rem(r + i, 16)
        remote(ar.at[q, 32:40], ar.at[q, 32:40], psend.at[0, 0], precv.at[q], mate).wait_recv()
        return carry

    lax.fori_loop(1, 16, wait_p, 0)
    cr[c] = jnp.sum(ar[:, 32:40], axis=0)

    def c_copy(i):
        return remote(cr.at[c], cr.at[c], csend.at[i], csrecv.at[c], (r, rem(c + i, 16)))

    for i in (8, 7, 9, 4, 12, 5, 11, 3, 13, 6, 10, 2, 14, 1, 15):
        c_copy(i).start()

    def b_copy(q):
        return remote(ar.at[q], tile.at[part], bsend.at[q], brecv.at[part], (r, q))

    def wait_a(q):
        remote(ar.at[q, 0:32], ar.at[q, 0:32], asend.at[0, 0], arecv.at[q], mate).wait_recv()

    def b_step(i, carry):
        q = rem(c + i, 16)

        @pl.when(q != r)
        def _():
            wait_a(q)

        @pl.when(i == 0)
        def _():
            tile[part] = ar[c]

        @pl.when(i > 0)
        def _():
            b_copy(q).start()

        return carry

    lax.fori_loop(0, 16, b_step, 0)

    def wait_c(i, carry):
        q = rem(c + i, 16)
        remote(cr.at[q], cr.at[q], csend.at[0], csrecv.at[q], mate).wait_recv()
        return carry

    lax.fori_loop(1, 16, wait_c, 0)
    both = jnp.sum(cr[...], axis=0)
    feat = decay_rate * fs[...] + (1.0 - decay_rate) * (both[1:2, :] / hid_count)
    feat_ref[...] = feat
    hid_mean = both[3:4, :] / hid_count
    tr[r] = jnp.full((1, 128), jnp.sum(both[2:3, :] / feat), jnp.float32)

    def t_copy(i):
        return remote(tr.at[r], tr.at[r], tsend.at[i], trecv.at[r], (rem(r + i, 16), c))

    for i in range(1, 16):
        t_copy(i).start()

    def drain(s, carry):
        first_copy(s, 1).wait_send()
        y_copy(s).wait_send()
        for kk in (0, 1):
            @pl.when(jnp.logical_not(mine(s, kk)))
            def _():
                a_copy(s, kk, r).wait_send()
                p_copy(s, kk, r).wait_send()
        mate_copy(s).wait_send()
        return carry

    lax.fori_loop(0, PAIRS, drain, 0)

    def drain_spans(t, carry):
        spans(t, lambda copy: copy.wait_send())
        return carry

    lax.fori_loop(2, STEPS - 2, drain_spans, 0)
    for one in sends.values():
        one.wait_send()

    @pl.when(jnp.logical_not(diagonal))
    def _():
        hx_copy.wait_send()

    def finish_b(i, carry):
        b_copy(rem(c + i, 16)).wait_send()
        c_copy(i).wait_send()
        q = rem(part + i, 16)
        remote(tile.at[q], tile.at[q], bsend.at[0], brecv.at[q], mate).wait_recv()
        return carry

    lax.fori_loop(1, 16, finish_b, 0)
    eye = lax.broadcasted_iota(jnp.int32, (128, 128), 0) == lax.broadcasted_iota(jnp.int32, (128, 128), 1)
    columns = []
    for q in range(4):
        line_q = tile[4 * q, 32:33] + tile[4 * q + 1, 32:33] + tile[4 * q + 2, 32:33] + tile[4 * q + 3, 32:33]
        hid_ref[q:q + 1, :] = line_q
        columns.append(lax.rsqrt(jnp.sum(jnp.where(eye, line_q, 0.0), axis=1, keepdims=True)))

    def wait_t(i, carry):
        q = rem(r + i, 16)
        remote(tr.at[q], tr.at[q], tsend.at[0], trecv.at[q], mate).wait_recv()
        t_copy(i).wait_send()
        return carry

    lax.fori_loop(1, 16, wait_t, 0)
    mean = hid_mean * jnp.sum(tr[...], axis=0) / (hid_count * feat_count)
    rms = jnp.sqrt(mean)
    rms_ref[...] = rms
    across = jnp.sqrt(hid_mean / feat) / jnp.maximum(1.0, rms)
    for q in range(4):
        g = tile[4 * q:4 * q + 4, 0:32].reshape(128, 128)
        upd_ref[128 * q:128 * q + 128, :] = g * columns[q] * across


def writer(a, b, c, d, oa, ob, oc, od, sem):
    copies = [pltpu.make_async_copy(src, dst, sem.at[i]) for i, (src, dst) in enumerate(((a, oa), (b, ob), (c, oc), (d, od)))]
    for copy in copies:
        copy.start()
    for copy in copies:
        copy.wait()


def body(layer_input, grad_output, hid_state, feat_state):
    tokens = layer_input.shape[0]
    hid_count, feat_count = 8192.0, 2048.0
    vm = pl.BlockSpec(memory_space=pltpu.VMEM)
    hbm = pl.BlockSpec(memory_space=pl.ANY)
    f32, bf16 = jnp.float32, jnp.bfloat16
    dma = pltpu.SemaphoreType.DMA
    shapes = (
        jax.ShapeDtypeStruct((512, 128), f32),
        jax.ShapeDtypeStruct((4, 128), f32),
        jax.ShapeDtypeStruct((1, 128), f32),
        jax.ShapeDtypeStruct((1, 128), f32),
    )
    outs = pl.pallas_call(
        functools.partial(kernel, tokens, hid_count, feat_count),
        name="optimizer_step",
        out_shape=shapes,
        in_specs=[hbm, hbm, hbm, hbm],
        out_specs=(vm, vm, vm, vm),
        scratch_shapes=[
            pltpu.VMEM((4, 1, 128), f32),
            pltpu.VMEM((1, 128), f32),
            pltpu.VMEM((1, 128), f32),
            pltpu.VMEM((tokens, 512), bf16),
            pltpu.VMEM((512, tokens), bf16),
            pltpu.VMEM((PAIRS, 2, tokens, 128), bf16),
            pltpu.VMEM((PAIRS, 512, 256), f32),
            pltpu.VMEM((PAIRS, TILE, 128), MSG),
            pltpu.VMEM((PAIRS, TILE, 128), MSG),
            pltpu.VMEM((STEPS, 2, 3 * TILE, 128), MSG),
            pltpu.VMEM((STEPS, 2, 3 * TILE, 128), MSG),
            pltpu.VMEM((PAIRS, 64, 256), f32),
            pltpu.VMEM((PAIRS, 32, 256), f32),
            pltpu.VMEM((PAIRS, 2, 32, 128), f32),
            pltpu.VMEM((PAIRS, 2, 8, 128), f32),
            pltpu.VMEM((16, 40, 128), f32),
            pltpu.VMEM((16, 40, 128), f32),
            pltpu.VMEM((32, 256), f32),
            pltpu.VMEM((16, 8, 128), f32),
            pltpu.VMEM((16, 1, 128), f32),
            dma((4,)), dma((16,)), dma((8,)), dma((PAIRS,)),
            dma((PAIRS,)), dma((PAIRS,)), dma((STEPS, 2)), dma((STEPS, 2)), dma((PAIRS,)), dma((PAIRS,)),
            dma((PAIRS, 2)), dma((16,)), dma((16,)), dma((16,)),
            dma((2,)), dma((PAIRS, 2)), dma((16,)), dma((16,)), dma((16,)), dma((16,)), dma((16,)),
        ],
        compiler_params=pltpu.CompilerParams(
            collective_id=0, has_side_effects=True, vmem_limit_bytes=62 << 20
        ),
    )(layer_input, grad_output, hid_state.reshape(4, 1, 128), feat_state.reshape(1, 128))
    update, hid, feat, rms = pl.pallas_call(
        writer,
        name="write_results",
        out_shape=shapes,
        in_specs=[vm] * 4,
        out_specs=[hbm] * 4,
        scratch_shapes=[dma((4,))],
        compiler_params=pltpu.CompilerParams(vmem_limit_bytes=62 << 20),
    )(*outs)
    return update, hid.reshape(512), feat.reshape(128), rms[0, 0]


def solution(mesh):
    in_specs = (P("col", "row"), P("col", "row"), P("col"), P("row"))
    out_specs = (P("col", "row"), P("col"), P("row"), P())
    return jax.shard_map(body, mesh=mesh, in_specs=in_specs, out_specs=out_specs, check_vma=False)
```

```python
import functools
import jax
import jax.numpy as jnp
from jax import lax
from jax.sharding import PartitionSpec as P
from jax.experimental import pallas as pl
from jax.experimental.pallas import tpu as pltpu

decay_rate = 0.8415106807538887
MESH = pl.DeviceIdType.MESH
PAIRS = 8
MSG = jnp.bfloat16
POWER = 13
LIFT = 2.0 ** 9
TILE = 144
PLAN = (
    (0, 0), (1, 0), (2, 0), (6, 0), (0, 1), (3, 0), (0, 2), (0, 3),
    (1, 1), (4, 0), (1, 2), (1, 3), (7, 0), (2, 1), (5, 0), (9, 0), (0, 4),
    (2, 2), (2, 3), (3, 1), (1, 4), (3, 2), (8, 5), (8, 6), (3, 3),
    (4, 1), (0, 5), (0, 6), (2, 4), (4, 2), (8, 7), (4, 3), (5, 1),
    (0, 7), (1, 5), (1, 6), (3, 4), (5, 2), (5, 3), (1, 7), (2, 5),
    (2, 6), (4, 4), (2, 7), (3, 5), (3, 6), (5, 4), (3, 7), (4, 5),
    (4, 6), (4, 7), (5, 5), (5, 6), (5, 7),
)


def rem(a, n):
    return lax.rem(a, n)


def encode(value):
    top = jnp.maximum(jnp.max(jnp.abs(value), axis=0, keepdims=True), 1e-30)
    scale = top.astype(MSG).astype(jnp.float32)
    m = value * (LIFT / scale)
    m2 = m * m
    m4 = m2 * m2
    coded = ((m * m4) * (m4 * m4)).astype(MSG)
    scales = [jnp.broadcast_to(scale[:, 128 * q:128 * q + 128], (8, 128)) for q in (0, 1)]
    return jnp.concatenate([coded[:, 0:128], coded[:, 128:256], jnp.concatenate(scales, axis=0).astype(MSG)], axis=0)


def decode(tile):
    scales = tile[128:144].astype(jnp.float32)
    parts = []
    for q in (0, 1):
        w = tile[64 * q:64 * q + 64].astype(jnp.float32)
        size = jnp.exp(jnp.log(jnp.maximum(jnp.abs(w), 1.2e-38)) * (1.0 / POWER))
        parts.append(jnp.where(w < 0.0, -size, size) * (scales[8 * q:8 * q + 1] * (1.0 / LIFT)))
    return jnp.concatenate(parts, axis=1)


def kernel(
    tokens, hid_count, feat_count,
    x_hbm, g_hbm, hs_hbm, fs_hbm,
    upd_ref, hid_ref, feat_ref, rms_ref,
    hs, hx, fs, gv, gt, xp, pb, sb, rb, fin, yr, ga, pm, ar, tile, racc, cr, tr,
    lsem, gsend, grecv, crecv, ssem, rsem, ysend, yrecv, asend, arecv, bsend, brecv,
    hsend, hrecv, psend, precv, csend, csrecv, tsend, trecv,
):
    r = lax.axis_index("row")
    c = lax.axis_index("col")
    x, yl, k = r // 4, rem(r // 2, 2), rem(r, 2)
    yh, z = c // 8, rem(c, 8)
    part = 2 * z + yh

    def row_of(dx, dy, kk):
        return rem(x + dx, 4) * 4 + rem(yl + dy, 2) * 2 + kk

    def remote(src, dst, send, recv, dev):
        return pltpu.make_async_remote_copy(
            src_ref=src, dst_ref=dst, send_sem=send, recv_sem=recv,
            device_id=dev, device_id_type=MESH,
        )

    copy_x = pltpu.make_async_copy(x_hbm, xp.at[0, k], lsem.at[0])
    copy_x.start()
    copy_g = pltpu.make_async_copy(g_hbm, gv, lsem.at[1])
    copy_g.start()
    copy_hs = pltpu.make_async_copy(hs_hbm, hs, lsem.at[2])
    copy_hs.start()
    copy_fs = pltpu.make_async_copy(fs_hbm, fs, lsem.at[3])
    copy_fs.start()

    barrier = pltpu.get_barrier_semaphore()
    diagonal = r == c
    east = (row_of(1, 0, k), c)
    west = (row_of(3, 0, k), c)
    side = (row_of(0, 1, k), c)
    mate = (row_of(0, 0, 1 - k), c)
    y_mate = (r, (1 - yh) * 8 + z)
    up = (r, yh * 8 + rem(z + 1, 8))
    down = (r, yh * 8 + rem(z + 7, 8))
    peers = (east, west, side, mate, y_mate, up, down)
    for dev in peers:
        pl.semaphore_signal(barrier, inc=1, device_id=dev, device_id_type=MESH)
    copy_x.wait()
    pl.semaphore_wait(barrier, len(peers))

    half = tokens // 2
    whole, low, high = pl.ds(0, tokens), pl.ds(0, half), pl.ds(half, half)

    def send_block(src_slot, dst_slot, rows, send, recv, dev):
        return remote(xp.at[src_slot, k, rows], xp.at[dst_slot, k, rows], gsend.at[send], grecv.at[recv], dev)

    def mate_copy(slot):
        return remote(xp.at[slot, k], xp.at[slot, k], gsend.at[8 + slot], crecv.at[slot], mate)

    sends = {
        "e0": send_block(0, 3, whole, 0, 3, east),
        "w0": send_block(0, 2, whole, 1, 2, west),
        "s0": send_block(0, 1, whole, 2, 1, side),
        "e1": send_block(1, 6, whole, 3, 6, east),
        "w1": send_block(1, 5, whole, 4, 5, west),
        "e3": send_block(3, 4, low, 5, 4, east),
        "w2": send_block(2, 4, high, 6, 0, west),
        "s4": send_block(4, 7, whole, 7, 7, side),
    }

    def wait_block(slot):
        if slot == 4:
            send_block(4, 4, low, 0, 4, east).wait_recv()
            send_block(4, 4, high, 0, 0, east).wait_recv()
        else:
            send_block(slot, slot, whole, 0, slot, east).wait_recv()

    def wait_mate(slot):
        remote(xp.at[slot, 1 - k], xp.at[slot, 1 - k], gsend.at[0], crecv.at[slot], mate).wait_recv()

    for name in ("e0", "w0", "s0"):
        sends[name].start()
    mate_copy(0).start()

    def hx_copy(i):
        to = rem(c + i, 16)
        return remote(hs.at[(2 * rem(to, 8) + to // 8) // 4], hx, hsend.at[i], hrecv, (r, to))

    copy_g.wait()
    copy_fs.wait()
    copy_hs.wait()
    gt[...] = gv[...].T
    racc[...] = jnp.zeros_like(racc)

    def z_dev(sign):
        return (r, yh * 8 + rem(z + sign + 8, 8))

    def message(s, m, sign):
        return remote(sb.at[s, m], rb.at[s, m], ssem.at[s, m], rsem.at[s, m], z_dev(sign))

    def chunk(s, offset):
        rows = pl.ds(pl.multiple_of(rem(z + offset + 8, 8) * 64, 64), 64)
        return pb[s, rows, :]

    def put(s, m, sign, value):
        sb[s, m] = encode(value)
        message(s, m, sign).start()

    def got(s, m):
        message(s, m, 1).wait_recv()
        return decode(rb[s, m])

    words = [sum((8 * kind + s) << (8 * i) for i, (kind, s) in enumerate(PLAN[at:at + 4])) for at in range(0, len(PLAN), 4)]

    def planned(t):
        word = jnp.int32(0)
        for i, value in enumerate(words):
            word = jnp.where(t // 4 == i, value, word)
        code = rem(lax.shift_right_logical(word, 8 * rem(t, 4)), 256)
        return code // 8, rem(code, 8)

    def slot_offset(p):
        dy = jnp.where(jnp.logical_or(p == 1, p >= 5), 1, 0)
        one = jnp.logical_or(p == 2, p == 5)
        three = jnp.logical_or(p == 3, p == 6)
        two = jnp.logical_or(p == 4, p == 7)
        dx = jnp.where(one, 1, 0) + jnp.where(two, 2, 0) + jnp.where(three, 3, 0)
        return dx, dy

    def y_copy(s):
        rows = pl.ds(pl.multiple_of((1 - yh) * 32, 32), 32)
        return remote(fin.at[s, rows], yr.at[s], ysend.at[s], yrecv.at[s], y_mate)

    def a_copy(s, kk, f):
        return remote(ga.at[s, kk], ar.at[r, 0:32], asend.at[s, kk], arecv.at[r], (f, c))

    def p_copy(s, kk, f):
        return remote(pm.at[s, kk], ar.at[r, 32:40], psend.at[s, kk], precv.at[r], (f, c))

    def mine(s, kk):
        return jnp.logical_and(s == 0, k == kk)

    def step(t, carry):
        kind, s = planned(t)

        @pl.when(kind == 0)
        def _():
            wait_mate(s)
            both = jnp.concatenate([xp[s, 0], xp[s, 1]], axis=1)
            pb[s] = jnp.dot(gt[...], both, preferred_element_type=jnp.float32)
            put(s, 0, 1 - 2 * rem(s, 2), chunk(s, 4))

        @pl.when(kind == 1)
        def _():
            for way, sign in ((0, 1), (1, -1)):
                long = rem(s, 2) == way

                @pl.when(long)
                def _():
                    put(s, 1 + way, sign, chunk(s, sign * 3) + got(s, 0))

                @pl.when(jnp.logical_not(long))
                def _():
                    put(s, 1 + way, sign, chunk(s, sign * 3))

        @pl.when(jnp.logical_or(kind == 2, kind == 3))
        def _():
            d = 4 - kind
            for way, sign in ((0, 1), (1, -1)):
                put(s, 7 - 2 * d + way, sign, chunk(s, sign * d) + got(s, 5 - 2 * d + way))

        @pl.when(kind == 4)
        def _():
            fin[s] = chunk(s, 0) + got(s, 5) + got(s, 6)
            y_copy(s).start()

        @pl.when(kind == 5)
        def _():
            y_copy(s).wait_recv()
            rows = pl.ds(pl.multiple_of(yh * 32, 32), 32)
            g = fin[s, rows, :] + yr[s]
            racc[...] += g * g + 1e-30
            dx, dy = slot_offset(s)
            for kk in (0, 1):
                ga[s, kk] = g[:, kk * 128:(kk + 1) * 128]

                @pl.when(mine(s, kk))
                def _():
                    ar[r, 0:32] = g[:, kk * 128:(kk + 1) * 128]

                @pl.when(jnp.logical_not(mine(s, kk)))
                def _():
                    a_copy(s, kk, row_of(dx, dy, kk)).start()

        @pl.when(kind == 6)
        def _():
            wait_block(1)
            mate_copy(1).start()
            wait_block(3)
            sends["e3"].start()
            mate_copy(3).start()
            wait_block(2)
            sends["w2"].start()
            mate_copy(2).start()
            sends["e1"].start()
            sends["w1"].start()

        @pl.when(kind == 7)
        def _():
            wait_block(4)
            sends["s4"].start()
            mate_copy(4).start()

        @pl.when(jnp.logical_and(kind == 9, diagonal))
        def _():
            hx[...] = hs[part // 4]
            for i in range(1, 16):
                hx_copy(i).start()

        @pl.when(kind == 8)
        def _():
            send_block(s, s, whole, 0, s, east).wait_recv()
            mate_copy(s).start()

        return carry

    lax.fori_loop(0, len(PLAN), step, 0)

    @pl.when(jnp.logical_not(diagonal))
    def _():
        hx_copy(1).wait_recv()

    sums = jnp.sum(racc[...], axis=1, keepdims=True)
    lane = lax.broadcasted_iota(jnp.int32, (32, 128), 1)
    line = lax.broadcasted_iota(jnp.int32, (32, 128), 0)
    place = lane == line + rem(part, 4) * 32
    old = jnp.sum(jnp.where(place, hx[...], 0.0), axis=1, keepdims=True)
    hid = decay_rate * old + (1.0 - decay_rate) * (sums / feat_count)
    hid_row = jnp.sum(jnp.where(place, hid, 0.0), axis=0, keepdims=True)
    hid_sum = jnp.full((1, 128), jnp.sum(hid), jnp.float32)
    inverse = 1.0 / hid

    def p_step(s, carry):
        dx, dy = slot_offset(s)
        for kk in (0, 1):
            sq = ga[s, kk] * ga[s, kk]
            pm[s, kk, 0:1] = hid_row
            pm[s, kk, 1:2] = jnp.sum(sq + 1e-30, axis=0, keepdims=True)
            pm[s, kk, 2:3] = jnp.sum(sq * inverse, axis=0, keepdims=True)
            pm[s, kk, 3:4] = hid_sum
            pm[s, kk, 4:8] = jnp.zeros((4, 128), jnp.float32)

            @pl.when(mine(s, kk))
            def _():
                ar[r, 32:40] = pm[s, kk]

            @pl.when(jnp.logical_not(mine(s, kk)))
            def _():
                p_copy(s, kk, row_of(dx, dy, kk)).start()

        return carry

    lax.fori_loop(0, PAIRS, p_step, 0)

    def drain(s, carry):
        for m in range(7):
            message(s, m, 1).wait_send()
        y_copy(s).wait_send()
        mate_copy(s).wait_send()
        for kk in (0, 1):
            @pl.when(jnp.logical_not(mine(s, kk)))
            def _():
                a_copy(s, kk, r).wait_send()

        return carry

    lax.fori_loop(0, PAIRS, drain, 0)
    for one in sends.values():
        one.wait_send()

    def wait_p(i, carry):
        q = rem(r + i, 16)
        remote(ar.at[q, 32:40], ar.at[q, 32:40], psend.at[0, 0], precv.at[q], mate).wait_recv()
        return carry

    lax.fori_loop(1, 16, wait_p, 0)
    cr[c] = jnp.sum(ar[:, 32:40], axis=0)

    def c_copy(i):
        return remote(cr.at[c], cr.at[c], csend.at[i], csrecv.at[c], (r, rem(c + i, 16)))

    for i in (8, 7, 9, 4, 12, 5, 11, 3, 13, 6, 10, 2, 14, 1, 15):
        c_copy(i).start()

    def b_copy(q):
        return remote(ar.at[q], tile.at[part], bsend.at[q], brecv.at[part], (r, q))

    def wait_a(q):
        remote(ar.at[q, 0:32], ar.at[q, 0:32], asend.at[0, 0], arecv.at[q], mate).wait_recv()

    def b_step(i, carry):
        q = rem(c + i, 16)

        @pl.when(q != r)
        def _():
            wait_a(q)

        @pl.when(i == 0)
        def _():
            tile[part] = ar[c]

        @pl.when(i > 0)
        def _():
            b_copy(q).start()

        return carry

    lax.fori_loop(0, 16, b_step, 0)

    def wait_c(i, carry):
        q = rem(c + i, 16)
        remote(cr.at[q], cr.at[q], csend.at[0], csrecv.at[q], mate).wait_recv()
        return carry

    lax.fori_loop(1, 16, wait_c, 0)
    both = jnp.sum(cr[...], axis=0)
    feat = decay_rate * fs[...] + (1.0 - decay_rate) * (both[1:2, :] / hid_count)
    feat_ref[...] = feat
    hid_mean = both[3:4, :] / hid_count
    tr[r] = jnp.full((1, 128), jnp.sum(both[2:3, :] / feat), jnp.float32)

    def t_copy(i):
        return remote(tr.at[r], tr.at[r], tsend.at[i], trecv.at[r], (rem(r + i, 16), c))

    for i in range(1, 16):
        t_copy(i).start()

    def drain_p(s, carry):
        for kk in (0, 1):
            @pl.when(jnp.logical_not(mine(s, kk)))
            def _():
                p_copy(s, kk, r).wait_send()

        return carry

    lax.fori_loop(0, PAIRS, drain_p, 0)

    @pl.when(diagonal)
    def _():
        for i in range(1, 16):
            hx_copy(i).wait_send()

    def finish_b(i, carry):
        b_copy(rem(c + i, 16)).wait_send()
        c_copy(i).wait_send()
        q = rem(part + i, 16)
        remote(tile.at[q], tile.at[q], bsend.at[0], brecv.at[q], mate).wait_recv()
        return carry

    lax.fori_loop(1, 16, finish_b, 0)
    eye = lax.broadcasted_iota(jnp.int32, (128, 128), 0) == lax.broadcasted_iota(jnp.int32, (128, 128), 1)
    columns = []
    for q in range(4):
        line_q = tile[4 * q, 32:33] + tile[4 * q + 1, 32:33] + tile[4 * q + 2, 32:33] + tile[4 * q + 3, 32:33]
        hid_ref[q:q + 1, :] = line_q
        columns.append(lax.rsqrt(jnp.sum(jnp.where(eye, line_q, 0.0), axis=1, keepdims=True)))

    def wait_t(i, carry):
        q = rem(r + i, 16)
        remote(tr.at[q], tr.at[q], tsend.at[0], trecv.at[q], mate).wait_recv()
        return carry

    lax.fori_loop(1, 16, wait_t, 0)
    for i in range(1, 16):
        t_copy(i).wait_send()
    mean = hid_mean * jnp.sum(tr[...], axis=0) / (hid_count * feat_count)
    rms = jnp.sqrt(mean)
    rms_ref[...] = rms
    across = jnp.sqrt(hid_mean / feat) / jnp.maximum(1.0, rms)
    for q in range(4):
        g = tile[4 * q:4 * q + 4, 0:32].reshape(128, 128)
        upd_ref[128 * q:128 * q + 128, :] = g * columns[q] * across


def writer(a, b, c, d, oa, ob, oc, od, sem):
    copies = [pltpu.make_async_copy(src, dst, sem.at[i]) for i, (src, dst) in enumerate(((a, oa), (b, ob), (c, oc), (d, od)))]
    for copy in copies:
        copy.start()
    for copy in copies:
        copy.wait()


def body(layer_input, grad_output, hid_state, feat_state):
    tokens = layer_input.shape[0]
    hid_count, feat_count = 8192.0, 2048.0
    vm = pl.BlockSpec(memory_space=pltpu.VMEM)
    hbm = pl.BlockSpec(memory_space=pl.ANY)
    f32, bf16 = jnp.float32, jnp.bfloat16
    dma = pltpu.SemaphoreType.DMA
    shapes = (
        jax.ShapeDtypeStruct((512, 128), f32),
        jax.ShapeDtypeStruct((4, 128), f32),
        jax.ShapeDtypeStruct((1, 128), f32),
        jax.ShapeDtypeStruct((1, 128), f32),
    )
    outs = pl.pallas_call(
        functools.partial(kernel, tokens, hid_count, feat_count),
        name="optimizer_step",
        out_shape=shapes,
        in_specs=[hbm, hbm, hbm, hbm],
        out_specs=(vm, vm, vm, vm),
        scratch_shapes=[
            pltpu.VMEM((4, 1, 128), f32),
            pltpu.VMEM((1, 128), f32),
            pltpu.VMEM((1, 128), f32),
            pltpu.VMEM((tokens, 512), bf16),
            pltpu.VMEM((512, tokens), bf16),
            pltpu.VMEM((PAIRS, 2, tokens, 128), bf16),
            pltpu.VMEM((PAIRS, 512, 256), f32),
            pltpu.VMEM((PAIRS, 7, TILE, 128), MSG),
            pltpu.VMEM((PAIRS, 7, TILE, 128), MSG),
            pltpu.VMEM((PAIRS, 64, 256), f32),
            pltpu.VMEM((PAIRS, 32, 256), f32),
            pltpu.VMEM((PAIRS, 2, 32, 128), f32),
            pltpu.VMEM((PAIRS, 2, 8, 128), f32),
            pltpu.VMEM((16, 40, 128), f32),
            pltpu.VMEM((16, 40, 128), f32),
            pltpu.VMEM((32, 256), f32),
            pltpu.VMEM((16, 8, 128), f32),
            pltpu.VMEM((16, 1, 128), f32),
            dma((4,)), dma((16,)), dma((8,)), dma((PAIRS,)),
            dma((PAIRS, 7)), dma((PAIRS, 7)), dma((PAIRS,)), dma((PAIRS,)),
            dma((PAIRS, 2)), dma((16,)), dma((16,)), dma((16,)),
            dma((16,)), dma, dma((PAIRS, 2)), dma((16,)), dma((16,)), dma((16,)), dma((16,)), dma((16,)),
        ],
        compiler_params=pltpu.CompilerParams(
            collective_id=0, has_side_effects=True, vmem_limit_bytes=62 << 20
        ),
    )(layer_input, grad_output, hid_state.reshape(4, 1, 128), feat_state.reshape(1, 128))
    update, hid, feat, rms = pl.pallas_call(
        writer,
        name="write_results",
        out_shape=shapes,
        in_specs=[vm] * 4,
        out_specs=[hbm] * 4,
        scratch_shapes=[dma((4,))],
        compiler_params=pltpu.CompilerParams(vmem_limit_bytes=62 << 20),
    )(*outs)
    return update, hid.reshape(512), feat.reshape(128), rms[0, 0]


def solution(mesh):
    in_specs = (P("col", "row"), P("col", "row"), P("col"), P("row"))
    out_specs = (P("col", "row"), P("col"), P("row"), P())
    return jax.shard_map(body, mesh=mesh, in_specs=in_specs, out_specs=out_specs, check_vma=False)
```

```python
import functools
import jax
import jax.numpy as jnp
from jax import lax
from jax.sharding import PartitionSpec as P
from jax.experimental import pallas as pl
from jax.experimental.pallas import tpu as pltpu

decay_rate = 0.8415106807538887
MESH = pl.DeviceIdType.MESH
PAIRS = 8
MSG = jnp.bfloat16
POWER = 13
LIFT = 2.0 ** 9
TILE = 144
HALF = 80
PLAN = (
    (0, 0), (1, 0), (6, 0), (2, 0), (7, 0), (0, 1), (0, 2), (0, 3),
    (10, 0), (8, 5), (3, 0), (1, 1), (0, 5), (1, 2), (8, 6), (8, 4),
    (1, 3), (2, 1), (0, 6), (0, 4), (2, 2), (8, 7), (2, 3), (1, 5),
    (0, 7), (1, 6), (1, 4), (3, 1), (2, 5), (1, 7), (2, 6), (2, 4),
    (3, 2), (3, 3), (2, 7), (3, 5), (3, 6), (3, 4), (4, 0), (9, 0),
    (4, 1), (3, 7), (4, 2), (4, 3), (4, 5), (4, 6), (4, 4), (4, 7),
)


def rem(a, n):
    return lax.rem(a, n)


def encode(value):
    top = jnp.maximum(jnp.max(jnp.abs(value), axis=0, keepdims=True), 1e-30)
    scale = top.astype(MSG).astype(jnp.float32)
    m = value * (LIFT / scale)
    m2 = m * m
    m4 = m2 * m2
    coded = ((m * m4) * (m4 * m4)).astype(MSG)
    scales = [jnp.broadcast_to(scale[:, 128 * q:128 * q + 128], (8, 128)) for q in (0, 1)]
    return jnp.concatenate([coded[:, 0:128], coded[:, 128:256], jnp.concatenate(scales, axis=0).astype(MSG)], axis=0)


def decode(tile):
    n = (tile.shape[0] - 16) // 2
    scales = tile[2 * n:2 * n + 16].astype(jnp.float32)
    parts = []
    for q in (0, 1):
        w = tile[n * q:n * q + n].astype(jnp.float32)
        size = jnp.exp(jnp.log(jnp.maximum(jnp.abs(w), 1.2e-38)) * (1.0 / POWER))
        parts.append(jnp.where(w < 0.0, -size, size) * (scales[8 * q:8 * q + 1] * (1.0 / LIFT)))
    return jnp.concatenate(parts, axis=1)


def kernel(
    tokens, hid_count, feat_count,
    x_hbm, g_hbm, hs_hbm, fs_hbm,
    upd_ref, hid_ref, feat_ref, rms_ref,
    hs, hx, fs, gv, gt, xp, pb, sb, rb, hsb, hrb, ga, fsum, pm, ar, tile, racc, cr, tr,
    lsem, gsend, grecv, msend, crecv, ssem, rsem, hssem, hrsem, asend, arecv, bsend, brecv,
    hsend, hrecv, psend, precv, csend, csrecv, tsend, trecv,
):
    r = lax.axis_index("row")
    c = lax.axis_index("col")
    x, yl, k = r // 4, rem(r // 2, 2), rem(r, 2)
    yh, z = c // 8, rem(c, 8)
    part = 2 * z + yh

    def row_of(dx, dy, kk):
        return rem(x + dx, 4) * 4 + rem(yl + dy, 2) * 2 + kk

    def remote(src, dst, send, recv, dev):
        return pltpu.make_async_remote_copy(
            src_ref=src, dst_ref=dst, send_sem=send, recv_sem=recv,
            device_id=dev, device_id_type=MESH,
        )

    copy_x = pltpu.make_async_copy(x_hbm, xp.at[0, k], lsem.at[0])
    copy_x.start()
    copy_g = pltpu.make_async_copy(g_hbm, gv, lsem.at[1])
    copy_g.start()
    copy_hs = pltpu.make_async_copy(hs_hbm, hs, lsem.at[2])
    copy_hs.start()
    copy_fs = pltpu.make_async_copy(fs_hbm, fs, lsem.at[3])
    copy_fs.start()

    barrier = pltpu.get_barrier_semaphore()
    diagonal = r == c
    east = (row_of(1, 0, k), c)
    west = (row_of(3, 0, k), c)
    side = (row_of(0, 1, k), c)
    mate = (row_of(0, 0, 1 - k), c)
    y_mate = (r, (1 - yh) * 8 + z)
    up = (r, yh * 8 + rem(z + 1, 8))
    down = (r, yh * 8 + rem(z + 7, 8))
    cross_up = (r, (1 - yh) * 8 + rem(z + 1, 8))
    cross_down = (r, (1 - yh) * 8 + rem(z + 7, 8))
    peers = (east, west, side, mate, y_mate, up, down, cross_up, cross_down)
    for dev in peers:
        pl.semaphore_signal(barrier, inc=1, device_id=dev, device_id_type=MESH)
    copy_x.wait()
    pl.semaphore_wait(barrier, len(peers))

    size = tokens // 4
    spans = {
        "a": pl.ds(0, tokens), "l": pl.ds(0, 2 * size), "h": pl.ds(2 * size, 2 * size),
        "l1": pl.ds(0, size), "l2": pl.ds(size, size), "h1": pl.ds(2 * size, size), "h2": pl.ds(3 * size, size),
    }
    routes = {
        "e0h": (0, 3, "h", east), "e0l": (0, 3, "l", east), "w0l": (0, 2, "l", west), "w0h": (0, 2, "h", west),
        "s0l1": (0, 1, "l1", side), "s0h1": (0, 1, "h1", side), "s0l2": (0, 1, "l2", side), "s0h2": (0, 1, "h2", side),
        "e1l1": (1, 6, "l1", east), "e1l2": (1, 6, "l2", east), "w1h1": (1, 5, "h1", west), "w1h2": (1, 5, "h2", west),
        "e3l": (3, 4, "l", east), "w2h": (2, 4, "h", west), "s2l": (2, 5, "l", side), "s3h": (3, 6, "h", side),
        "e6l": (6, 7, "l", east), "w5h": (5, 7, "h", west),
    }
    number = {name: i for i, name in enumerate(routes)}
    arrives = {(there, rows): number[name] for name, (_, there, rows, _) in routes.items()}

    def block_copy(name):
        here, there, rows, dev = routes[name]
        i = number[name]
        return remote(xp.at[here, k, spans[rows]], xp.at[there, k, spans[rows]], gsend, grecv.at[i], dev)

    def forward(*names):
        for name in names:
            block_copy(name).start()

    def wait_rows(slot, *rows):
        for one in rows:
            i = arrives[slot, one]
            ref = xp.at[slot, k, spans[one]]
            remote(ref, ref, gsend, grecv.at[i], mate).wait_recv()

    def mate_copy(slot):
        return remote(xp.at[slot, k], xp.at[slot, k], msend, crecv.at[slot], mate)

    def wait_mate(slot):
        remote(xp.at[slot, 1 - k], xp.at[slot, 1 - k], msend, crecv.at[slot], mate).wait_recv()

    forward("e0h", "w0l", "s0l1", "s0h1", "e0l", "w0h", "s0l2", "s0h2")
    mate_copy(0).start()

    def hx_copy(i):
        to = rem(c + i, 16)
        return remote(hs.at[(2 * rem(to, 8) + to // 8) // 4], hx, hsend, hrecv, (r, to))

    copy_g.wait()
    copy_fs.wait()
    copy_hs.wait()
    gt[...] = gv[...].T
    racc[...] = jnp.zeros_like(racc)

    def z_dev(sign):
        return (r, yh * 8 + rem(z + sign + 8, 8))

    def message(s, m, sign):
        return remote(sb.at[s, m], rb.at[s, m], ssem, rsem.at[s, m], z_dev(sign))

    def chunk(s, offset):
        rows = pl.ds(pl.multiple_of(rem(z + offset + 8, 8) * 64, 64), 64)
        return pb[s, rows, :]

    def put(s, m, sign, value):
        sb[s, m] = encode(value)
        message(s, m, sign).start()

    def got(s, m):
        message(s, m, 1).wait_recv()
        return decode(rb[s, m])

    words = [sum((8 * kind + s) << (8 * i) for i, (kind, s) in enumerate(PLAN[at:at + 4])) for at in range(0, len(PLAN), 4)]

    def planned(t):
        word = jnp.int32(0)
        for i, value in enumerate(words):
            word = jnp.where(t // 4 == i, value, word)
        code = rem(lax.shift_right_logical(word, 8 * rem(t, 4)), 256)
        return code // 8, rem(code, 8)

    def slot_offset(p):
        dy = jnp.where(jnp.logical_or(p == 1, p >= 5), 1, 0)
        one = jnp.logical_or(p == 2, p == 5)
        three = jnp.logical_or(p == 3, p == 6)
        two = jnp.logical_or(p == 4, p == 7)
        dx = jnp.where(one, 1, 0) + jnp.where(two, 2, 0) + jnp.where(three, 3, 0)
        return dx, dy

    def half_copy(s, way, q):
        to = (r, q * 8 + rem(z + 9 - 2 * way, 8))
        return remote(hsb.at[s, 2 * way + q], hrb.at[s, 2 * way + yh], hssem, hrsem.at[s, 2 * way + yh], to)

    def y_copy(s):
        return remote(hsb.at[s, 4], hrb.at[s, 4], hssem, hrsem.at[s, 4], y_mate)

    def got_half(s, i):
        remote(hsb.at[s, i], hrb.at[s, i], hssem, hrsem.at[s, i], y_mate).wait_recv()
        return decode(hrb[s, i])

    def own_rows(s, q):
        return pb[s, pl.ds(pl.multiple_of(z * 64 + q * 32, 32), 32), :]

    def a_copy(s, kk, f):
        return remote(ga.at[s, kk], ar.at[r, 0:32], asend, arecv, (f, c))

    def p_copy(s, kk, f):
        return remote(pm.at[s, kk], ar.at[r, 32:40], psend, precv, (f, c))

    def mine(s, kk):
        return jnp.logical_and(s == 0, k == kk)

    def step(t, carry):
        kind, s = planned(t)

        @pl.when(kind == 0)
        def _():
            wait_mate(s)
            both = jnp.concatenate([xp[s, 0], xp[s, 1]], axis=1)
            pb[s] = jnp.dot(gt[...], both, preferred_element_type=jnp.float32)
            put(s, 0, 1 - 2 * rem(s, 2), chunk(s, 4))
            hsb[s, 4] = encode(own_rows(s, 1 - yh))
            y_copy(s).start()

        @pl.when(kind == 1)
        def _():
            for way, sign in ((0, 1), (1, -1)):
                long = rem(s, 2) == way

                @pl.when(long)
                def _():
                    put(s, 1 + way, sign, chunk(s, sign * 3) + got(s, 0))

                @pl.when(jnp.logical_not(long))
                def _():
                    put(s, 1 + way, sign, chunk(s, sign * 3))

        @pl.when(kind == 2)
        def _():
            for way, sign in ((0, 1), (1, -1)):
                put(s, 3 + way, sign, chunk(s, sign * 2) + got(s, 1 + way))

        @pl.when(kind == 3)
        def _():
            for way, sign in ((0, 1), (1, -1)):
                value = chunk(s, sign) + got(s, 3 + way)
                for q in (0, 1):
                    hsb[s, 2 * way + q] = encode(value[32 * q:32 * q + 32])
                    half_copy(s, way, q).start()

        @pl.when(kind == 4)
        def _():
            g = own_rows(s, yh)
            for i in (4, 0, 1, 2, 3):
                g = g + got_half(s, i)
            squares = g * g + 1e-30
            racc[...] += squares
            dx, dy = slot_offset(s)
            for kk in (0, 1):
                ga[s, kk] = g[:, kk * 128:(kk + 1) * 128]
                fsum[s, kk] = jnp.sum(squares[:, kk * 128:(kk + 1) * 128], axis=0, keepdims=True)

                @pl.when(mine(s, kk))
                def _():
                    ar[r, 0:32] = g[:, kk * 128:(kk + 1) * 128]

                @pl.when(jnp.logical_not(mine(s, kk)))
                def _():
                    a_copy(s, kk, row_of(dx, dy, kk)).start()

        @pl.when(kind == 6)
        def _():
            wait_rows(1, "l1", "h1")
            forward("e1l1", "w1h1")
            wait_rows(2, "l")
            forward("s2l")
            wait_rows(3, "h")
            forward("s3h")

        @pl.when(kind == 7)
        def _():
            wait_rows(1, "l2", "h2")
            forward("e1l2", "w1h2")
            wait_rows(3, "l")
            forward("e3l")
            wait_rows(2, "h")
            forward("w2h")
            for slot in (1, 2, 3):
                mate_copy(slot).start()

        @pl.when(kind == 10)
        def _():
            wait_rows(6, "l1", "l2")
            forward("e6l")
            wait_rows(5, "h1", "h2")
            forward("w5h")

        for slot, rows in ((4, ("l", "h")), (5, ("l",)), (6, ("h",)), (7, ("l", "h"))):
            @pl.when(jnp.logical_and(kind == 8, s == slot))
            def _():
                wait_rows(slot, *rows)
                mate_copy(slot).start()

        @pl.when(jnp.logical_and(kind == 9, diagonal))
        def _():
            hx[...] = hs[part // 4]
            for i in range(1, 16):
                hx_copy(i).start()

        return carry

    lax.fori_loop(0, len(PLAN), step, 0)

    @pl.when(jnp.logical_not(diagonal))
    def _():
        hx_copy(1).wait_recv()

    sums = jnp.sum(racc[...], axis=1, keepdims=True)
    lane = lax.broadcasted_iota(jnp.int32, (32, 128), 1)
    line = lax.broadcasted_iota(jnp.int32, (32, 128), 0)
    place = lane == line + rem(part, 4) * 32
    old = jnp.sum(jnp.where(place, hx[...], 0.0), axis=1, keepdims=True)
    hid = decay_rate * old + (1.0 - decay_rate) * (sums / feat_count)
    hid_row = jnp.sum(jnp.where(place, hid, 0.0), axis=0, keepdims=True)
    hid_sum = jnp.full((1, 128), jnp.sum(hid), jnp.float32)
    inverse = 1.0 / hid

    for s in range(PAIRS):
        for kk in (0, 1):
            weighted = jnp.sum(ga[s, kk] * ga[s, kk] * inverse, axis=0, keepdims=True)
            pm[s, kk] = jnp.concatenate([hid_row, fsum[s, kk], weighted, hid_sum, jnp.zeros((4, 128), jnp.float32)], axis=0)
            if s == 0:
                @pl.when(k == kk)
                def _():
                    ar[r, 32:40] = pm[s, kk]

                @pl.when(k != kk)
                def _():
                    p_copy(s, kk, row_of(*slot_offset(s), kk)).start()
            else:
                p_copy(s, kk, row_of(*slot_offset(s), kk)).start()

    def left(ref, sem):
        remote(ref, ref, sem, sem, mate).wait_send()

    def came(ref, sem):
        remote(ref, ref, sem, sem, mate).wait_recv()

    left(sb, ssem)
    left(hsb, hssem)
    left(xp.at[:, 0], msend)
    left(xp.at[0:7, 0], gsend)
    left(ar.at[0:15, 0:32], asend)
    came(cr.at[0:15], precv)
    cr[c] = jnp.sum(ar[:, 32:40], axis=0)

    def c_copy(i):
        return remote(cr.at[c], cr.at[c], csend, csrecv, (r, rem(c + i, 16)))

    for i in (8, 7, 9, 4, 12, 5, 11, 3, 13, 6, 10, 2, 14, 1, 15):
        c_copy(i).start()

    def b_copy(q):
        return remote(ar.at[q], tile.at[part], bsend, brecv, (r, q))

    came(ar.at[0:15, 0:32], arecv)
    tile[part] = ar[c]
    for i in range(1, 16):
        b_copy(rem(c + i, 16)).start()
    left(cr.at[0:15], psend)

    @pl.when(diagonal)
    def _():
        left(tr.at[0:15], hsend)

    came(cr.at[0:15], csrecv)
    both = jnp.sum(cr[...], axis=0)
    feat = decay_rate * fs[...] + (1.0 - decay_rate) * (both[1:2, :] / hid_count)
    feat_ref[...] = feat
    hid_mean = both[3:4, :] / hid_count
    tr[r] = jnp.full((1, 128), jnp.sum(both[2:3, :] / feat), jnp.float32)

    def t_copy(i):
        return remote(tr.at[r], tr.at[r], tsend, trecv, (rem(r + i, 16), c))

    for i in (12, 4, 8, 13, 14, 15, 9, 10, 11, 5, 6, 7, 3, 2, 1):
        t_copy(i).start()

    came(tile.at[0:15], brecv)
    left(cr.at[0:15], csend)
    left(ar.at[0:15], bsend)
    eye = lax.broadcasted_iota(jnp.int32, (128, 128), 0) == lax.broadcasted_iota(jnp.int32, (128, 128), 1)
    columns = []
    for q in range(4):
        line_q = tile[4 * q, 32:33] + tile[4 * q + 1, 32:33] + tile[4 * q + 2, 32:33] + tile[4 * q + 3, 32:33]
        hid_ref[q:q + 1, :] = line_q
        columns.append(lax.rsqrt(jnp.sum(jnp.where(eye, line_q, 0.0), axis=1, keepdims=True)))

    across0 = jnp.sqrt(hid_mean / feat)
    came(tr.at[0:15], trecv)
    mean = hid_mean * jnp.sum(tr[...], axis=0) / (hid_count * feat_count)
    rms = jnp.sqrt(mean)
    rms_ref[...] = rms
    across = across0 / jnp.maximum(1.0, rms)
    for q in range(4):
        g = tile[4 * q:4 * q + 4, 0:32].reshape(128, 128)
        upd_ref[128 * q:128 * q + 128, :] = g * columns[q] * across

    left(tr.at[0:15], tsend)


def writer(a, b, c, d, oa, ob, oc, od, sem):
    copies = [pltpu.make_async_copy(src, dst, sem.at[i]) for i, (src, dst) in enumerate(((a, oa), (b, ob), (c, oc), (d, od)))]
    for copy in copies:
        copy.start()
    for copy in copies:
        copy.wait()


def body(layer_input, grad_output, hid_state, feat_state):
    tokens = layer_input.shape[0]
    hid_count, feat_count = 8192.0, 2048.0
    vm = pl.BlockSpec(memory_space=pltpu.VMEM)
    hbm = pl.BlockSpec(memory_space=pl.ANY)
    f32, bf16 = jnp.float32, jnp.bfloat16
    dma = pltpu.SemaphoreType.DMA
    shapes = (
        jax.ShapeDtypeStruct((512, 128), f32),
        jax.ShapeDtypeStruct((4, 128), f32),
        jax.ShapeDtypeStruct((1, 128), f32),
        jax.ShapeDtypeStruct((1, 128), f32),
    )
    outs = pl.pallas_call(
        functools.partial(kernel, tokens, hid_count, feat_count),
        name="optimizer_step",
        out_shape=shapes,
        in_specs=[hbm, hbm, hbm, hbm],
        out_specs=(vm, vm, vm, vm),
        scratch_shapes=[
            pltpu.VMEM((4, 1, 128), f32),
            pltpu.VMEM((1, 128), f32),
            pltpu.VMEM((1, 128), f32),
            pltpu.VMEM((tokens, 512), bf16),
            pltpu.VMEM((512, tokens), bf16),
            pltpu.VMEM((PAIRS, 2, tokens, 128), bf16),
            pltpu.VMEM((PAIRS, 512, 256), f32),
            pltpu.VMEM((PAIRS, 5, TILE, 128), MSG),
            pltpu.VMEM((PAIRS, 5, TILE, 128), MSG),
            pltpu.VMEM((PAIRS, 5, HALF, 128), MSG),
            pltpu.VMEM((PAIRS, 5, HALF, 128), MSG),
            pltpu.VMEM((PAIRS, 2, 32, 128), f32),
            pltpu.VMEM((PAIRS, 2, 1, 128), f32),
            pltpu.VMEM((PAIRS, 2, 8, 128), f32),
            pltpu.VMEM((16, 40, 128), f32),
            pltpu.VMEM((16, 40, 128), f32),
            pltpu.VMEM((32, 256), f32),
            pltpu.VMEM((16, 8, 128), f32),
            pltpu.VMEM((16, 1, 128), f32),
            dma((4,)), dma, dma((18,)), dma, dma((PAIRS,)),
            dma, dma((PAIRS, 5)), dma, dma((PAIRS, 5)), dma, dma, dma, dma,
            dma, dma, dma, dma, dma, dma, dma, dma,
        ],
        compiler_params=pltpu.CompilerParams(
            collective_id=0, has_side_effects=True, vmem_limit_bytes=62 << 20
        ),
    )(layer_input, grad_output, hid_state.reshape(4, 1, 128), feat_state.reshape(1, 128))
    update, hid, feat, rms = pl.pallas_call(
        writer,
        name="write_results",
        out_shape=shapes,
        in_specs=[vm] * 4,
        out_specs=[hbm] * 4,
        scratch_shapes=[dma((4,))],
        compiler_params=pltpu.CompilerParams(vmem_limit_bytes=62 << 20),
    )(*outs)
    return update, hid.reshape(512), feat.reshape(128), rms[0, 0]


def solution(mesh):
    in_specs = (P("col", "row"), P("col", "row"), P("col"), P("row"))
    out_specs = (P("col", "row"), P("col"), P("row"), P())
    return jax.shard_map(body, mesh=mesh, in_specs=in_specs, out_specs=out_specs, check_vma=False)
```

```python
import functools
import jax
import jax.numpy as jnp
from jax import lax
from jax.sharding import PartitionSpec as P
from jax.experimental import pallas as pl
from jax.experimental.pallas import tpu as pltpu

decay_rate = 0.8415106807538887
MESH = pl.DeviceIdType.MESH
PAIRS = 8
MSG = jnp.bfloat16
POWER = 13
LIFT = 2.0 ** 9
TILE = 144
HALF = 80
PLAN = (
    (0, 0), (1, 0), (6, 0), (2, 0), (7, 0), (0, 1), (0, 2), (0, 3),
    (10, 0), (8, 5), (3, 0), (1, 1), (0, 5), (1, 2), (8, 6), (8, 4),
    (1, 3), (2, 1), (0, 6), (0, 4), (2, 2), (8, 7), (2, 3), (1, 5),
    (0, 7), (1, 6), (1, 4), (3, 1), (2, 5), (1, 7), (2, 6), (2, 4),
    (3, 2), (3, 3), (2, 7), (3, 5), (3, 6), (3, 4), (4, 0), (9, 0),
    (4, 1), (3, 7), (4, 2), (4, 3), (4, 5), (4, 6), (4, 4), (4, 7),
)


def rem(a, n):
    return lax.rem(a, n)


def encode(value):
    top = jnp.maximum(jnp.max(jnp.abs(value), axis=0, keepdims=True), 1e-30)
    scale = top.astype(MSG).astype(jnp.float32)
    m = value * (LIFT / scale)
    m2 = m * m
    m4 = m2 * m2
    coded = ((m * m4) * (m4 * m4)).astype(MSG)
    scales = [jnp.broadcast_to(scale[:, 128 * q:128 * q + 128], (8, 128)) for q in (0, 1)]
    return jnp.concatenate([coded[:, 0:128], coded[:, 128:256], jnp.concatenate(scales, axis=0).astype(MSG)], axis=0)


def decode(tile):
    n = (tile.shape[0] - 16) // 2
    scales = tile[2 * n:2 * n + 16].astype(jnp.float32)
    parts = []
    for q in (0, 1):
        w = tile[n * q:n * q + n].astype(jnp.float32)
        size = jnp.exp(jnp.log(jnp.maximum(jnp.abs(w), 1.2e-38)) * (1.0 / POWER))
        parts.append(jnp.where(w < 0.0, -size, size) * (scales[8 * q:8 * q + 1] * (1.0 / LIFT)))
    return jnp.concatenate(parts, axis=1)


def kernel(
    tokens, hid_count, feat_count,
    x_hbm, g_hbm, hs_hbm, fs_hbm,
    upd_ref, hid_ref, feat_ref, rms_ref,
    hs, hx, fs, gv, gt, xp, pb, sb, rb, hsb, hrb, ga, fsum, pm, ar, tile, racc, cr, tr,
    lsem, gsend, grecv, msend, crecv, ssem, rsem, hssem, hrsem, asend, arecv, bsend, brecv,
    hsend, hrecv, psend, precv, csend, csrecv, tsend, trecv,
):
    r = lax.axis_index("row")
    c = lax.axis_index("col")
    x, yl, k = r // 4, rem(r // 2, 2), rem(r, 2)
    yh, z = c // 8, rem(c, 8)
    part = 2 * z + yh

    def row_of(dx, dy, kk):
        return rem(x + dx, 4) * 4 + rem(yl + dy, 2) * 2 + kk

    def remote(src, dst, send, recv, dev):
        return pltpu.make_async_remote_copy(
            src_ref=src, dst_ref=dst, send_sem=send, recv_sem=recv,
            device_id=dev, device_id_type=MESH,
        )

    copy_x = pltpu.make_async_copy(x_hbm, xp.at[0, k], lsem.at[0])
    copy_x.start()
    copy_g = pltpu.make_async_copy(g_hbm, gv, lsem.at[1])
    copy_g.start()
    copy_hs = pltpu.make_async_copy(hs_hbm, hs, lsem.at[2])
    copy_hs.start()
    copy_fs = pltpu.make_async_copy(fs_hbm, fs, lsem.at[3])
    copy_fs.start()

    barrier = pltpu.get_barrier_semaphore()
    diagonal = r == c
    east = (row_of(1, 0, k), c)
    west = (row_of(3, 0, k), c)
    side = (row_of(0, 1, k), c)
    mate = (row_of(0, 0, 1 - k), c)
    y_mate = (r, (1 - yh) * 8 + z)
    up = (r, yh * 8 + rem(z + 1, 8))
    down = (r, yh * 8 + rem(z + 7, 8))
    cross_up = (r, (1 - yh) * 8 + rem(z + 1, 8))
    cross_down = (r, (1 - yh) * 8 + rem(z + 7, 8))
    peers = (east, west, side, mate, y_mate, up, down, cross_up, cross_down)
    for dev in peers:
        pl.semaphore_signal(barrier, inc=1, device_id=dev, device_id_type=MESH)
    copy_x.wait()
    pl.semaphore_wait(barrier, len(peers))

    size = tokens // 4
    spans = {
        "a": pl.ds(0, tokens), "l": pl.ds(0, 2 * size), "h": pl.ds(2 * size, 2 * size),
        "l1": pl.ds(0, size), "l2": pl.ds(size, size), "h1": pl.ds(2 * size, size), "h2": pl.ds(3 * size, size),
    }
    routes = {
        "e0h": (0, 3, "h", east), "e0l": (0, 3, "l", east), "w0l": (0, 2, "l", west), "w0h": (0, 2, "h", west),
        "s0l1": (0, 1, "l1", side), "s0h1": (0, 1, "h1", side), "s0l2": (0, 1, "l2", side), "s0h2": (0, 1, "h2", side),
        "e1l1": (1, 6, "l1", east), "e1l2": (1, 6, "l2", east), "w1h1": (1, 5, "h1", west), "w1h2": (1, 5, "h2", west),
        "e3l": (3, 4, "l", east), "w2h": (2, 4, "h", west), "s2l": (2, 5, "l", side), "s3h": (3, 6, "h", side),
        "e6l": (6, 7, "l", east), "w5h": (5, 7, "h", west),
    }
    number = {name: i for i, name in enumerate(routes)}
    arrives = {(there, rows): number[name] for name, (_, there, rows, _) in routes.items()}

    def block_copy(name):
        here, there, rows, dev = routes[name]
        i = number[name]
        return remote(xp.at[here, k, spans[rows]], xp.at[there, k, spans[rows]], gsend, grecv.at[i], dev)

    def forward(*names):
        for name in names:
            block_copy(name).start()

    def wait_rows(slot, *rows):
        for one in rows:
            i = arrives[slot, one]
            ref = xp.at[slot, k, spans[one]]
            remote(ref, ref, gsend, grecv.at[i], mate).wait_recv()

    def mate_copy(slot):
        return remote(xp.at[slot, k], xp.at[slot, k], msend, crecv.at[slot], mate)

    def wait_mate(slot):
        remote(xp.at[slot, 1 - k], xp.at[slot, 1 - k], msend, crecv.at[slot], mate).wait_recv()

    forward("e0h", "w0l", "s0l1", "s0h1", "e0l", "w0h", "s0l2", "s0h2")
    mate_copy(0).start()

    def hx_copy(i):
        to = rem(c + i, 16)
        return remote(hs.at[(2 * rem(to, 8) + to // 8) // 4], hx, hsend, hrecv, (r, to))

    copy_g.wait()
    copy_fs.wait()
    copy_hs.wait()
    gt[...] = gv[...].T
    racc[...] = jnp.zeros_like(racc)

    def z_dev(sign):
        return (r, yh * 8 + rem(z + sign + 8, 8))

    def message(s, m, sign):
        return remote(sb.at[s, m], rb.at[s, m], ssem, rsem.at[s, m], z_dev(sign))

    def chunk(s, offset):
        rows = pl.ds(pl.multiple_of(rem(z + offset + 8, 8) * 64, 64), 64)
        return pb[s, rows, :]

    def put(s, m, sign, value):
        sb[s, m] = encode(value)
        message(s, m, sign).start()

    def got(s, m):
        message(s, m, 1).wait_recv()
        return decode(rb[s, m])

    words = [sum((8 * kind + s) << (8 * i) for i, (kind, s) in enumerate(PLAN[at:at + 4])) for at in range(0, len(PLAN), 4)]

    def planned(t):
        word = jnp.int32(0)
        for i, value in enumerate(words):
            word = jnp.where(t // 4 == i, value, word)
        code = rem(lax.shift_right_logical(word, 8 * rem(t, 4)), 256)
        return code // 8, rem(code, 8)

    def slot_offset(p):
        dy = jnp.where(jnp.logical_or(p == 1, p >= 5), 1, 0)
        one = jnp.logical_or(p == 2, p == 5)
        three = jnp.logical_or(p == 3, p == 6)
        two = jnp.logical_or(p == 4, p == 7)
        dx = jnp.where(one, 1, 0) + jnp.where(two, 2, 0) + jnp.where(three, 3, 0)
        return dx, dy

    def half_copy(s, way, q):
        to = (r, q * 8 + rem(z + 9 - 2 * way, 8))
        return remote(hsb.at[s, 2 * way + q], hrb.at[s, 2 * way + yh], hssem, hrsem.at[s, 2 * way + yh], to)

    def y_copy(s):
        return remote(hsb.at[s, 4], hrb.at[s, 4], hssem, hrsem.at[s, 4], y_mate)

    def got_half(s, i):
        remote(hsb.at[s, i], hrb.at[s, i], hssem, hrsem.at[s, i], y_mate).wait_recv()
        return decode(hrb[s, i])

    def own_rows(s, q):
        return pb[s, pl.ds(pl.multiple_of(z * 64 + q * 32, 32), 32), :]

    def a_copy(s, kk, f):
        return remote(ga.at[s, kk], ar.at[r, 0:32], asend, arecv, (f, c))

    def p_copy(s, kk, f):
        return remote(pm.at[s, kk], ar.at[r, 32:40], psend, precv, (f, c))

    def mine(s, kk):
        return jnp.logical_and(s == 0, k == kk)

    def step(t, carry):
        kind, s = planned(t)

        @pl.when(kind == 0)
        def _():
            wait_mate(s)
            both = jnp.concatenate([xp[s, 0], xp[s, 1]], axis=1)
            pb[s] = jnp.dot(gt[...], both, preferred_element_type=jnp.float32)
            put(s, 0, 1 - 2 * rem(s, 2), chunk(s, 4))
            hsb[s, 4] = encode(own_rows(s, 1 - yh))
            y_copy(s).start()

        @pl.when(kind == 1)
        def _():
            for way, sign in ((0, 1), (1, -1)):
                long = rem(s, 2) == way

                @pl.when(long)
                def _():
                    put(s, 1 + way, sign, chunk(s, sign * 3) + got(s, 0))

                @pl.when(jnp.logical_not(long))
                def _():
                    put(s, 1 + way, sign, chunk(s, sign * 3))

        @pl.when(kind == 2)
        def _():
            for way, sign in ((0, 1), (1, -1)):
                put(s, 3 + way, sign, chunk(s, sign * 2) + got(s, 1 + way))

        @pl.when(kind == 3)
        def _():
            for way, sign in ((0, 1), (1, -1)):
                value = chunk(s, sign) + got(s, 3 + way)
                for q in (0, 1):
                    hsb[s, 2 * way + q] = encode(value[32 * q:32 * q + 32])
                    half_copy(s, way, q).start()

        @pl.when(kind == 4)
        def _():
            g = own_rows(s, yh)
            for i in (4, 0, 1, 2, 3):
                g = g + got_half(s, i)
            squares = g * g + 1e-30
            racc[...] += squares
            dx, dy = slot_offset(s)
            for kk in (0, 1):
                ga[s, kk] = g[:, kk * 128:(kk + 1) * 128]
                fsum[s, kk] = jnp.sum(squares[:, kk * 128:(kk + 1) * 128], axis=0, keepdims=True)

                @pl.when(mine(s, kk))
                def _():
                    ar[r, 0:32] = g[:, kk * 128:(kk + 1) * 128]

                @pl.when(jnp.logical_not(mine(s, kk)))
                def _():
                    a_copy(s, kk, row_of(dx, dy, kk)).start()

        @pl.when(kind == 6)
        def _():
            wait_rows(1, "l1", "h1")
            forward("e1l1", "w1h1")
            wait_rows(2, "l")
            forward("s2l")
            wait_rows(3, "h")
            forward("s3h")

        @pl.when(kind == 7)
        def _():
            wait_rows(1, "l2", "h2")
            forward("e1l2", "w1h2")
            wait_rows(3, "l")
            forward("e3l")
            wait_rows(2, "h")
            forward("w2h")
            for slot in (1, 2, 3):
                mate_copy(slot).start()

        @pl.when(kind == 10)
        def _():
            wait_rows(6, "l1", "l2")
            forward("e6l")
            wait_rows(5, "h1", "h2")
            forward("w5h")

        for slot, rows in ((4, ("l", "h")), (5, ("l",)), (6, ("h",)), (7, ("l", "h"))):
            @pl.when(jnp.logical_and(kind == 8, s == slot))
            def _():
                wait_rows(slot, *rows)
                mate_copy(slot).start()

        @pl.when(jnp.logical_and(kind == 9, diagonal))
        def _():
            hx[...] = hs[part // 4]
            for i in range(1, 16):
                hx_copy(i).start()

        return carry

    lax.fori_loop(0, len(PLAN), step, 0)

    @pl.when(jnp.logical_not(diagonal))
    def _():
        hx_copy(1).wait_recv()

    sums = jnp.sum(racc[...], axis=1, keepdims=True)
    lane = lax.broadcasted_iota(jnp.int32, (32, 128), 1)
    line = lax.broadcasted_iota(jnp.int32, (32, 128), 0)
    place = lane == line + rem(part, 4) * 32
    old = jnp.sum(jnp.where(place, hx[...], 0.0), axis=1, keepdims=True)
    hid = decay_rate * old + (1.0 - decay_rate) * (sums / feat_count)
    hid_row = jnp.sum(jnp.where(place, hid, 0.0), axis=0, keepdims=True)
    hid_sum = jnp.full((1, 128), jnp.sum(hid), jnp.float32)
    inverse = 1.0 / hid

    for s in range(PAIRS):
        for kk in (0, 1):
            weighted = jnp.sum(ga[s, kk] * ga[s, kk] * inverse, axis=0, keepdims=True)
            pm[s, kk] = jnp.concatenate([hid_row, fsum[s, kk], weighted, hid_sum, jnp.zeros((4, 128), jnp.float32)], axis=0)
            if s == 0:
                @pl.when(k == kk)
                def _():
                    ar[r, 32:40] = pm[s, kk]

                @pl.when(k != kk)
                def _():
                    p_copy(s, kk, row_of(*slot_offset(s), kk)).start()
            else:
                p_copy(s, kk, row_of(*slot_offset(s), kk)).start()

    def left(ref, sem):
        remote(ref, ref, sem, sem, mate).wait_send()

    def came(ref, sem):
        remote(ref, ref, sem, sem, mate).wait_recv()

    left(sb, ssem)
    left(hsb, hssem)
    left(xp.at[:, 0], msend)
    left(xp.at[0:7, 0], gsend)
    left(ar.at[0:15, 0:32], asend)
    came(cr.at[0:15], precv)
    cr[c] = jnp.sum(ar[:, 32:40], axis=0)

    def c_copy(i):
        return remote(cr.at[c], cr.at[c], csend, csrecv, (r, rem(c + i, 16)))

    for i in (8, 7, 9, 4, 12, 5, 11, 3, 13, 6, 10, 2, 14, 1, 15):
        c_copy(i).start()

    def b_copy(q):
        return remote(ar.at[q], tile.at[part], bsend, brecv, (r, q))

    came(ar.at[0:15, 0:32], arecv)
    tile[part] = ar[c]
    for i in range(1, 16):
        b_copy(rem(c + i, 16)).start()
    left(cr.at[0:15], psend)

    @pl.when(diagonal)
    def _():
        left(tr.at[0:15], hsend)

    came(cr.at[0:15], csrecv)
    both = jnp.sum(cr[...], axis=0)
    feat = decay_rate * fs[...] + (1.0 - decay_rate) * (both[1:2, :] / hid_count)
    feat_ref[...] = feat
    hid_mean = both[3:4, :] / hid_count
    tr[r] = jnp.full((1, 128), jnp.sum(both[2:3, :] / feat), jnp.float32)

    def t_copy(i):
        return remote(tr.at[r], tr.at[r], tsend, trecv, (rem(r + i, 16), c))

    for i in (12, 4, 8, 13, 14, 15, 9, 10, 11, 5, 6, 7, 3, 2, 1):
        t_copy(i).start()

    came(tile.at[0:15], brecv)
    left(cr.at[0:15], csend)
    left(ar.at[0:15], bsend)
    eye = lax.broadcasted_iota(jnp.int32, (128, 128), 0) == lax.broadcasted_iota(jnp.int32, (128, 128), 1)
    columns = []
    for q in range(4):
        line_q = tile[4 * q, 32:33] + tile[4 * q + 1, 32:33] + tile[4 * q + 2, 32:33] + tile[4 * q + 3, 32:33]
        hid_ref[q:q + 1, :] = line_q
        columns.append(lax.rsqrt(jnp.sum(jnp.where(eye, line_q, 0.0), axis=1, keepdims=True)))

    across0 = jnp.sqrt(hid_mean / feat)
    came(tr.at[0:15], trecv)
    mean = hid_mean * jnp.sum(tr[...], axis=0) / (hid_count * feat_count)
    rms = jnp.sqrt(mean)
    rms_ref[...] = rms
    across = across0 / jnp.maximum(1.0, rms)
    for q in range(4):
        g = tile[4 * q:4 * q + 4, 0:32].reshape(128, 128)
        upd_ref[128 * q:128 * q + 128, :] = g * columns[q] * across

    left(tr.at[0:15], tsend)


def writer(a, b, c, d, oa, ob, oc, od, sem):
    copies = [pltpu.make_async_copy(src, dst, sem.at[i]) for i, (src, dst) in enumerate(((a, oa), (b, ob), (c, oc), (d, od)))]
    for copy in copies:
        copy.start()
    for copy in copies:
        copy.wait()


def body(layer_input, grad_output, hid_state, feat_state):
    tokens = layer_input.shape[0]
    hid_count, feat_count = 8192.0, 2048.0
    vm = pl.BlockSpec(memory_space=pltpu.VMEM)
    hbm = pl.BlockSpec(memory_space=pl.ANY)
    f32, bf16 = jnp.float32, jnp.bfloat16
    dma = pltpu.SemaphoreType.DMA
    shapes = (
        jax.ShapeDtypeStruct((512, 128), f32),
        jax.ShapeDtypeStruct((4, 128), f32),
        jax.ShapeDtypeStruct((1, 128), f32),
        jax.ShapeDtypeStruct((1, 128), f32),
    )
    outs = pl.pallas_call(
        functools.partial(kernel, tokens, hid_count, feat_count),
        name="optimizer_step",
        out_shape=tuple(pltpu.VMEM(one.shape, one.dtype) for one in shapes),
        in_specs=[pl.BlockSpec(memory_space=pltpu.HBM)] * 4,
        out_specs=(vm, vm, vm, vm),
        scratch_shapes=[
            pltpu.VMEM((4, 1, 128), f32),
            pltpu.VMEM((1, 128), f32),
            pltpu.VMEM((1, 128), f32),
            pltpu.VMEM((tokens, 512), bf16),
            pltpu.VMEM((512, tokens), bf16),
            pltpu.VMEM((PAIRS, 2, tokens, 128), bf16),
            pltpu.VMEM((PAIRS, 512, 256), f32),
            pltpu.VMEM((PAIRS, 5, TILE, 128), MSG),
            pltpu.VMEM((PAIRS, 5, TILE, 128), MSG),
            pltpu.VMEM((PAIRS, 5, HALF, 128), MSG),
            pltpu.VMEM((PAIRS, 5, HALF, 128), MSG),
            pltpu.VMEM((PAIRS, 2, 32, 128), f32),
            pltpu.VMEM((PAIRS, 2, 1, 128), f32),
            pltpu.VMEM((PAIRS, 2, 8, 128), f32),
            pltpu.VMEM((16, 40, 128), f32),
            pltpu.VMEM((16, 40, 128), f32),
            pltpu.VMEM((32, 256), f32),
            pltpu.VMEM((16, 8, 128), f32),
            pltpu.VMEM((16, 1, 128), f32),
            dma((4,)), dma, dma((18,)), dma, dma((PAIRS,)),
            dma, dma((PAIRS, 5)), dma, dma((PAIRS, 5)), dma, dma, dma, dma,
            dma, dma, dma, dma, dma, dma, dma, dma,
        ],
        compiler_params=pltpu.CompilerParams(
            collective_id=0, has_side_effects=True, vmem_limit_bytes=62 << 20
        ),
    )(layer_input, grad_output, hid_state.reshape(4, 1, 128), feat_state.reshape(1, 128))
    update, hid, feat, rms = pl.pallas_call(
        writer,
        name="write_results",
        out_shape=shapes,
        in_specs=[vm] * 4,
        out_specs=[pl.BlockSpec(memory_space=pltpu.HBM)] * 4,
        scratch_shapes=[dma((4,))],
        compiler_params=pltpu.CompilerParams(vmem_limit_bytes=1 << 20),
    )(*outs)
    return update, hid.reshape(512), feat.reshape(128), rms[0, 0]


def solution(mesh):
    in_specs = (P("col", "row"), P("col", "row"), P("col"), P("row"))
    out_specs = (P("col", "row"), P("col"), P("row"), P())
    return jax.shard_map(body, mesh=mesh, in_specs=in_specs, out_specs=out_specs, check_vma=False)
```

```python
import functools
import jax
import jax.numpy as jnp
from jax import lax
from jax.sharding import PartitionSpec as P
from jax.experimental import pallas as pl
from jax.experimental.pallas import tpu as pltpu

decay_rate = 0.8415106807538887
MESH = pl.DeviceIdType.MESH
PAIRS = 8
MSG = jnp.bfloat16
POWER = 13
LIFT = 2.0 ** 9
TILE = 144
HALF = 80
PLAN = (
    (0, 0), (1, 0), (6, 0), (2, 0), (7, 0), (0, 1), (0, 2), (0, 3),
    (10, 0), (8, 5), (3, 0), (1, 1), (0, 5), (1, 2), (8, 6), (8, 4),
    (1, 3), (2, 1), (0, 6), (0, 4), (2, 2), (8, 7), (2, 3), (1, 5),
    (0, 7), (1, 6), (1, 4), (3, 1), (2, 5), (1, 7), (2, 6), (2, 4),
    (3, 2), (3, 3), (2, 7), (3, 5), (3, 6), (3, 4), (4, 0), (9, 0),
    (4, 1), (3, 7), (4, 2), (4, 3), (4, 5), (4, 6), (4, 4), (4, 7),
)


def rem(a, n):
    return lax.rem(a, n)


def encode(value):
    top = jnp.maximum(jnp.max(jnp.abs(value), axis=0, keepdims=True), 1e-30)
    scale = top.astype(MSG).astype(jnp.float32)
    m = value * (LIFT / scale)
    m2 = m * m
    m4 = m2 * m2
    coded = ((m * m4) * (m4 * m4)).astype(MSG)
    scales = [jnp.broadcast_to(scale[:, 128 * q:128 * q + 128], (8, 128)) for q in (0, 1)]
    return jnp.concatenate([coded[:, 0:128], coded[:, 128:256], jnp.concatenate(scales, axis=0).astype(MSG)], axis=0)


def decode(tile):
    n = (tile.shape[0] - 16) // 2
    scales = tile[2 * n:2 * n + 16].astype(jnp.float32)
    parts = []
    for q in (0, 1):
        w = tile[n * q:n * q + n].astype(jnp.float32)
        size = jnp.exp(jnp.log(jnp.maximum(jnp.abs(w), 1.2e-38)) * (1.0 / POWER))
        parts.append(jnp.where(w < 0.0, -size, size) * (scales[8 * q:8 * q + 1] * (1.0 / LIFT)))
    return jnp.concatenate(parts, axis=1)


def kernel(
    tokens, hid_count, feat_count,
    x_hbm, g_hbm, hs_hbm, fs_hbm,
    upd_ref, hid_ref, feat_ref, rms_ref,
    hs, hx, fs, gv, gt, xp, pb, sb, rb, hsb, hrb, ga, fsum, pm, ar, tile, pr, cm, racc, cr, tr,
    lsem, gsend, grecv, msend, crecv, ssem, rsem, hssem, hrsem, asend, arecv, bsend, brecv,
    hsend, hrecv, psend, precv, csend, csrecv, tsend, trecv,
):
    r = lax.axis_index("row")
    c = lax.axis_index("col")
    x, yl, k = r // 4, rem(r // 2, 2), rem(r, 2)
    yh, z = c // 8, rem(c, 8)
    part = 2 * z + yh

    def row_of(dx, dy, kk):
        return rem(x + dx, 4) * 4 + rem(yl + dy, 2) * 2 + kk

    def remote(src, dst, send, recv, dev):
        return pltpu.make_async_remote_copy(
            src_ref=src, dst_ref=dst, send_sem=send, recv_sem=recv,
            device_id=dev, device_id_type=MESH,
        )

    copy_x = pltpu.make_async_copy(x_hbm, xp.at[0, k], lsem.at[0])
    copy_x.start()
    copy_g = pltpu.make_async_copy(g_hbm, gv, lsem.at[1])
    copy_g.start()
    copy_hs = pltpu.make_async_copy(hs_hbm, hs, lsem.at[2])
    copy_hs.start()
    copy_fs = pltpu.make_async_copy(fs_hbm, fs, lsem.at[3])
    copy_fs.start()

    barrier = pltpu.get_barrier_semaphore()
    diagonal = r == c
    east = (row_of(1, 0, k), c)
    west = (row_of(3, 0, k), c)
    side = (row_of(0, 1, k), c)
    mate = (row_of(0, 0, 1 - k), c)
    y_mate = (r, (1 - yh) * 8 + z)
    up = (r, yh * 8 + rem(z + 1, 8))
    down = (r, yh * 8 + rem(z + 7, 8))
    cross_up = (r, (1 - yh) * 8 + rem(z + 1, 8))
    cross_down = (r, (1 - yh) * 8 + rem(z + 7, 8))
    peers = (cross_up, cross_down, y_mate, east, west, side, up, down, mate)
    for dev in peers:
        pl.semaphore_signal(barrier, inc=1, device_id=dev, device_id_type=MESH)
    copy_x.wait()
    pl.semaphore_wait(barrier, len(peers))

    size = tokens // 4
    spans = {
        "a": pl.ds(0, tokens), "l": pl.ds(0, 2 * size), "h": pl.ds(2 * size, 2 * size),
        "l1": pl.ds(0, size), "l2": pl.ds(size, size), "h1": pl.ds(2 * size, size), "h2": pl.ds(3 * size, size),
    }
    routes = {
        "e0h": (0, 3, "h", east), "e0l": (0, 3, "l", east), "w0l": (0, 2, "l", west), "w0h": (0, 2, "h", west),
        "s0l1": (0, 1, "l1", side), "s0h1": (0, 1, "h1", side), "s0l2": (0, 1, "l2", side), "s0h2": (0, 1, "h2", side),
        "e1l1": (1, 6, "l1", east), "e1l2": (1, 6, "l2", east), "w1h1": (1, 5, "h1", west), "w1h2": (1, 5, "h2", west),
        "e3l": (3, 4, "l", east), "w2h": (2, 4, "h", west), "s2l": (2, 5, "l", side), "s3h": (3, 6, "h", side),
        "e6l": (6, 7, "l", east), "w5h": (5, 7, "h", west),
    }
    number = {name: i for i, name in enumerate(routes)}
    arrives = {(there, rows): number[name] for name, (_, there, rows, _) in routes.items()}

    def block_copy(name):
        here, there, rows, dev = routes[name]
        i = number[name]
        return remote(xp.at[here, k, spans[rows]], xp.at[there, k, spans[rows]], gsend, grecv.at[i], dev)

    def forward(*names):
        for name in names:
            block_copy(name).start()

    def wait_rows(slot, *rows):
        for one in rows:
            i = arrives[slot, one]
            ref = xp.at[slot, k, spans[one]]
            remote(ref, ref, gsend, grecv.at[i], mate).wait_recv()

    def mate_copy(slot):
        return remote(xp.at[slot, k], xp.at[slot, k], msend, crecv.at[slot], mate)

    def wait_mate(slot):
        remote(xp.at[slot, 1 - k], xp.at[slot, 1 - k], msend, crecv.at[slot], mate).wait_recv()

    forward("e0h", "w0l", "s0l1", "s0h1", "e0l", "w0h", "s0l2", "s0h2")
    mate_copy(0).start()

    def hx_copy(i):
        to = rem(c + i, 16)
        return remote(hs.at[(2 * rem(to, 8) + to // 8) // 4], hx, hsend, hrecv, (r, to))

    copy_g.wait()
    copy_fs.wait()
    copy_hs.wait()
    gt[...] = gv[...].T
    racc[...] = jnp.zeros_like(racc)

    def z_dev(sign):
        return (r, yh * 8 + rem(z + sign + 8, 8))

    def message(s, m, sign):
        return remote(sb.at[s, m], rb.at[s, m], ssem, rsem.at[s, m], z_dev(sign))

    def chunk(s, offset):
        rows = pl.ds(pl.multiple_of(rem(z + offset + 8, 8) * 64, 64), 64)
        return pb[s, rows, :]

    def put(s, m, sign, value):
        sb[s, m] = encode(value)
        message(s, m, sign).start()

    def got(s, m):
        message(s, m, 1).wait_recv()
        return decode(rb[s, m])

    words = [sum((8 * kind + s) << (8 * i) for i, (kind, s) in enumerate(PLAN[at:at + 4])) for at in range(0, len(PLAN), 4)]

    def planned(t):
        word = jnp.int32(0)
        for i, value in enumerate(words):
            word = jnp.where(t // 4 == i, value, word)
        code = rem(lax.shift_right_logical(word, 8 * rem(t, 4)), 256)
        return code // 8, rem(code, 8)

    def slot_offset(p):
        dy = jnp.where(jnp.logical_or(p == 1, p >= 5), 1, 0)
        one = jnp.logical_or(p == 2, p == 5)
        three = jnp.logical_or(p == 3, p == 6)
        two = jnp.logical_or(p == 4, p == 7)
        dx = jnp.where(one, 1, 0) + jnp.where(two, 2, 0) + jnp.where(three, 3, 0)
        return dx, dy

    def half_copy(s, way, q):
        to = (r, q * 8 + rem(z + 9 - 2 * way, 8))
        return remote(hsb.at[s, 2 * way + q], hrb.at[s, 2 * way + yh], hssem, hrsem.at[s, 2 * way + yh], to)

    def y_copy(s):
        return remote(hsb.at[s, 4], hrb.at[s, 4], hssem, hrsem.at[s, 4], y_mate)

    def got_half(s, i):
        remote(hsb.at[s, i], hrb.at[s, i], hssem, hrsem.at[s, i], y_mate).wait_recv()
        return decode(hrb[s, i])

    def own_rows(s, q):
        return pb[s, pl.ds(pl.multiple_of(z * 64 + q * 32, 32), 32), :]

    def a_copy(s, kk, f):
        return remote(ga.at[s, kk], ar.at[r], asend, arecv, (f, c))

    def p_copy(s, kk, f):
        return remote(pm.at[s, kk], pr.at[r], psend, precv, (f, c))

    def mine(s, kk):
        return jnp.logical_and(s == 0, k == kk)

    def step(t, carry):
        kind, s = planned(t)

        @pl.when(kind == 0)
        def _():
            wait_mate(s)
            both = jnp.concatenate([xp[s, 0], xp[s, 1]], axis=1)
            pb[s] = jnp.dot(gt[...], both, preferred_element_type=jnp.float32)
            put(s, 0, 1 - 2 * rem(s, 2), chunk(s, 4))

        @pl.when(kind == 1)
        def _():
            for way, sign in ((0, 1), (1, -1)):
                long = rem(s, 2) == way

                @pl.when(long)
                def _():
                    put(s, 1 + way, sign, chunk(s, sign * 3) + got(s, 0))

                @pl.when(jnp.logical_not(long))
                def _():
                    put(s, 1 + way, sign, chunk(s, sign * 3))

            hsb[s, 4] = encode(own_rows(s, 1 - yh))
            y_copy(s).start()

        @pl.when(kind == 2)
        def _():
            for way, sign in ((0, 1), (1, -1)):
                put(s, 3 + way, sign, chunk(s, sign * 2) + got(s, 1 + way))

        @pl.when(kind == 3)
        def _():
            for way, sign in ((0, 1), (1, -1)):
                value = chunk(s, sign) + got(s, 3 + way)
                for q in (0, 1):
                    hsb[s, 2 * way + q] = encode(value[32 * q:32 * q + 32])
                    half_copy(s, way, q).start()

        @pl.when(kind == 4)
        def _():
            g = own_rows(s, yh)
            for i in (4, 0, 1, 2, 3):
                g = g + got_half(s, i)
            squares = g * g + 1e-30
            racc[...] += squares
            dx, dy = slot_offset(s)
            for kk in (0, 1):
                ga[s, kk] = g[:, kk * 128:(kk + 1) * 128]
                fsum[s, kk] = jnp.sum(squares[:, kk * 128:(kk + 1) * 128], axis=0, keepdims=True)

                @pl.when(mine(s, kk))
                def _():
                    ar[r] = g[:, kk * 128:(kk + 1) * 128]

                @pl.when(jnp.logical_not(mine(s, kk)))
                def _():
                    a_copy(s, kk, row_of(dx, dy, kk)).start()

        @pl.when(kind == 6)
        def _():
            wait_rows(1, "l1", "h1")
            forward("e1l1", "w1h1")
            wait_rows(2, "l")
            forward("s2l")
            wait_rows(3, "h")
            forward("s3h")

        @pl.when(kind == 7)
        def _():
            wait_rows(1, "l2", "h2")
            forward("e1l2", "w1h2")
            wait_rows(3, "l")
            forward("e3l")
            wait_rows(2, "h")
            forward("w2h")
            for slot in (1, 2, 3):
                mate_copy(slot).start()

        @pl.when(kind == 10)
        def _():
            wait_rows(6, "l1", "l2")
            forward("e6l")
            wait_rows(5, "h1", "h2")
            forward("w5h")

        for slot, rows in ((4, ("l", "h")), (5, ("l",)), (6, ("h",)), (7, ("l", "h"))):
            @pl.when(jnp.logical_and(kind == 8, s == slot))
            def _():
                wait_rows(slot, *rows)
                mate_copy(slot).start()

        @pl.when(jnp.logical_and(kind == 9, diagonal))
        def _():
            hx[...] = hs[part // 4]
            for i in range(1, 16):
                hx_copy(i).start()

        return carry

    lax.fori_loop(0, len(PLAN), step, 0)

    @pl.when(jnp.logical_not(diagonal))
    def _():
        hx_copy(1).wait_recv()

    sums = jnp.sum(racc[...], axis=1, keepdims=True)
    lane = lax.broadcasted_iota(jnp.int32, (32, 128), 1)
    line = lax.broadcasted_iota(jnp.int32, (32, 128), 0)
    place = lane == line + rem(part, 4) * 32
    old = jnp.sum(jnp.where(place, hx[...], 0.0), axis=1, keepdims=True)
    hid = decay_rate * old + (1.0 - decay_rate) * (sums / feat_count)
    hid_row = jnp.sum(jnp.where(place, hid, 0.0), axis=0, keepdims=True)
    hid_sum = jnp.full((1, 128), jnp.sum(hid), jnp.float32)
    inverse = 1.0 / hid

    for s in range(PAIRS):
        for kk in (0, 1):
            weighted = jnp.sum(ga[s, kk] * ga[s, kk] * inverse, axis=0, keepdims=True)
            pm[s, kk] = jnp.concatenate([hid_row, fsum[s, kk], weighted, hid_sum, jnp.zeros((4, 128), jnp.float32)], axis=0)
            if s == 0:
                @pl.when(k == kk)
                def _():
                    pr[r] = pm[s, kk]

                @pl.when(k != kk)
                def _():
                    p_copy(s, kk, row_of(*slot_offset(s), kk)).start()
            else:
                p_copy(s, kk, row_of(*slot_offset(s), kk)).start()

    def left(ref, sem):
        remote(ref, ref, sem, sem, mate).wait_send()

    def came(ref, sem):
        remote(ref, ref, sem, sem, mate).wait_recv()

    left(sb, ssem)
    left(hsb, hssem)
    left(xp.at[:, 0], msend)
    left(xp.at[0:7, 0], gsend)
    left(ar.at[0:15], asend)
    came(cr.at[0:15], precv)
    totals = jnp.sum(pr[...], axis=0)
    top = lax.broadcasted_iota(jnp.int32, (8, 128), 0) == 0
    for q in range(16):
        cm[q] = jnp.where(top, pr[q], totals)
    cr[part] = cm[c]

    def c_copy(i):
        q = rem(c + i, 16)
        return remote(cm.at[q], cr.at[part], csend, csrecv, (r, q))

    for i in (8, 7, 9, 4, 12, 5, 11, 3, 13, 6, 10, 2, 14, 1, 15):
        c_copy(i).start()

    def b_copy(q):
        return remote(ar.at[q], tile.at[part], bsend, brecv, (r, q))

    came(ar.at[0:15], arecv)
    tile[part] = ar[c]
    for i in range(1, 16):
        b_copy(rem(c + i, 16)).start()
    left(cr.at[0:15], psend)

    @pl.when(diagonal)
    def _():
        left(tr.at[0:15], hsend)

    came(cr.at[0:15], csrecv)
    both = jnp.sum(cr[...], axis=0)
    feat = decay_rate * fs[...] + (1.0 - decay_rate) * (both[1:2, :] / hid_count)
    feat_ref[...] = feat
    hid_mean = both[3:4, :] / hid_count
    tr[r] = jnp.full((1, 128), jnp.sum(both[2:3, :] / feat), jnp.float32)

    def t_copy(i):
        return remote(tr.at[r], tr.at[r], tsend, trecv, (rem(r + i, 16), c))

    for i in (12, 4, 8, 13, 14, 15, 9, 10, 11, 5, 6, 7, 3, 2, 1):
        t_copy(i).start()

    eye = lax.broadcasted_iota(jnp.int32, (128, 128), 0) == lax.broadcasted_iota(jnp.int32, (128, 128), 1)
    columns = []
    for q in range(4):
        line_q = cr[4 * q, 0:1] + cr[4 * q + 1, 0:1] + cr[4 * q + 2, 0:1] + cr[4 * q + 3, 0:1]
        hid_ref[q:q + 1, :] = line_q
        columns.append(lax.rsqrt(jnp.sum(jnp.where(eye, line_q, 0.0), axis=1, keepdims=True)))

    across0 = jnp.sqrt(hid_mean / feat)
    came(tile.at[0:15], brecv)
    left(cr.at[0:15], csend)
    left(ar.at[0:15], bsend)
    came(tr.at[0:15], trecv)
    mean = hid_mean * jnp.sum(tr[...], axis=0) / (hid_count * feat_count)
    rms = jnp.sqrt(mean)
    rms_ref[...] = rms
    across = across0 / jnp.maximum(1.0, rms)
    for q in range(4):
        g = tile[4 * q:4 * q + 4].reshape(128, 128)
        upd_ref[128 * q:128 * q + 128, :] = g * columns[q] * across

    left(tr.at[0:15], tsend)


def writer(a, b, c, d, oa, ob, oc, od, sem):
    copies = [pltpu.make_async_copy(src, dst, sem.at[i]) for i, (src, dst) in enumerate(((a, oa), (b, ob), (c, oc), (d, od)))]
    for copy in copies:
        copy.start()
    for copy in copies:
        copy.wait()


def body(layer_input, grad_output, hid_state, feat_state):
    tokens = layer_input.shape[0]
    hid_count, feat_count = 8192.0, 2048.0
    vm = pl.BlockSpec(memory_space=pltpu.VMEM)
    hbm = pl.BlockSpec(memory_space=pl.ANY)
    f32, bf16 = jnp.float32, jnp.bfloat16
    dma = pltpu.SemaphoreType.DMA
    shapes = (
        jax.ShapeDtypeStruct((512, 128), f32),
        jax.ShapeDtypeStruct((4, 128), f32),
        jax.ShapeDtypeStruct((1, 128), f32),
        jax.ShapeDtypeStruct((1, 128), f32),
    )
    outs = pl.pallas_call(
        functools.partial(kernel, tokens, hid_count, feat_count),
        name="optimizer_step",
        out_shape=tuple(pltpu.VMEM(one.shape, one.dtype) for one in shapes),
        in_specs=[pl.BlockSpec(memory_space=pltpu.HBM)] * 4,
        out_specs=(vm, vm, vm, vm),
        scratch_shapes=[
            pltpu.VMEM((4, 1, 128), f32),
            pltpu.VMEM((1, 128), f32),
            pltpu.VMEM((1, 128), f32),
            pltpu.VMEM((tokens, 512), bf16),
            pltpu.VMEM((512, tokens), bf16),
            pltpu.VMEM((PAIRS, 2, tokens, 128), bf16),
            pltpu.VMEM((PAIRS, 512, 256), f32),
            pltpu.VMEM((PAIRS, 5, TILE, 128), MSG),
            pltpu.VMEM((PAIRS, 5, TILE, 128), MSG),
            pltpu.VMEM((PAIRS, 5, HALF, 128), MSG),
            pltpu.VMEM((PAIRS, 5, HALF, 128), MSG),
            pltpu.VMEM((PAIRS, 2, 32, 128), f32),
            pltpu.VMEM((PAIRS, 2, 1, 128), f32),
            pltpu.VMEM((PAIRS, 2, 8, 128), f32),
            pltpu.VMEM((16, 32, 128), f32),
            pltpu.VMEM((16, 32, 128), f32),
            pltpu.VMEM((16, 8, 128), f32),
            pltpu.VMEM((16, 8, 128), f32),
            pltpu.VMEM((32, 256), f32),
            pltpu.VMEM((16, 8, 128), f32),
            pltpu.VMEM((16, 1, 128), f32),
            dma((4,)), dma, dma((18,)), dma, dma((PAIRS,)),
            dma, dma((PAIRS, 5)), dma, dma((PAIRS, 5)), dma, dma, dma, dma,
            dma, dma, dma, dma, dma, dma, dma, dma,
        ],
        compiler_params=pltpu.CompilerParams(
            collective_id=0, has_side_effects=True, vmem_limit_bytes=62 << 20
        ),
    )(layer_input, grad_output, hid_state.reshape(4, 1, 128), feat_state.reshape(1, 128))
    update, hid, feat, rms = pl.pallas_call(
        writer,
        name="write_results",
        out_shape=shapes,
        in_specs=[vm] * 4,
        out_specs=[pl.BlockSpec(memory_space=pltpu.HBM)] * 4,
        scratch_shapes=[dma((4,))],
        compiler_params=pltpu.CompilerParams(vmem_limit_bytes=1 << 20),
    )(*outs)
    return update, hid.reshape(512), feat.reshape(128), rms[0, 0]


def solution(mesh):
    in_specs = (P("col", "row"), P("col", "row"), P("col"), P("row"))
    out_specs = (P("col", "row"), P("col"), P("row"), P())
    return jax.shard_map(body, mesh=mesh, in_specs=in_specs, out_specs=out_specs, check_vma=False)
```

```python
import functools
import jax
import jax.numpy as jnp
from jax import lax
from jax.sharding import PartitionSpec as P
from jax.experimental import pallas as pl
from jax.experimental.pallas import tpu as pltpu

decay_rate = 0.8415106807538887
MESH = pl.DeviceIdType.MESH
PAIRS = 8
MSG = jnp.bfloat16
POWER = 13
LIFT = 2.0 ** 9
TILE = 144
HALF = 80
PLAN = (
    (0, 0), (1, 0), (6, 0), (2, 0), (7, 0), (0, 1), (0, 2), (0, 3),
    (10, 0), (8, 5), (3, 0), (1, 1), (0, 5), (1, 2), (8, 6), (8, 4),
    (1, 3), (2, 1), (0, 6), (0, 4), (2, 2), (8, 7), (2, 3), (1, 5),
    (0, 7), (1, 6), (1, 4), (3, 1), (2, 5), (1, 7), (2, 6), (2, 4),
    (3, 2), (3, 3), (2, 7), (3, 5), (3, 6), (3, 4), (4, 0), (9, 0),
    (4, 1), (3, 7), (4, 2), (4, 3), (4, 5), (4, 6), (4, 4), (4, 7),
)


def rem(a, n):
    return a % n if isinstance(a, int) else lax.rem(a, n)


def encode(value):
    top = jnp.maximum(jnp.max(jnp.abs(value), axis=0, keepdims=True), 1e-30)
    scale = top.astype(MSG).astype(jnp.float32)
    m = value * (LIFT / scale)
    m2 = m * m
    m4 = m2 * m2
    coded = ((m * m4) * (m4 * m4)).astype(MSG)
    scales = [jnp.broadcast_to(scale[:, 128 * q:128 * q + 128], (8, 128)) for q in (0, 1)]
    return jnp.concatenate([coded[:, 0:128], coded[:, 128:256], jnp.concatenate(scales, axis=0).astype(MSG)], axis=0)


def decode(tile):
    n = (tile.shape[0] - 16) // 2
    scales = tile[2 * n:2 * n + 16].astype(jnp.float32)
    parts = []
    for q in (0, 1):
        w = tile[n * q:n * q + n].astype(jnp.float32)
        size = jnp.exp(jnp.log(jnp.maximum(jnp.abs(w), 1.2e-38)) * (1.0 / POWER))
        parts.append(jnp.where(w < 0.0, -size, size) * (scales[8 * q:8 * q + 1] * (1.0 / LIFT)))
    return jnp.concatenate(parts, axis=1)


def kernel(
    tokens, hid_count, feat_count,
    x_hbm, g_hbm, hs_hbm, fs_hbm,
    upd_ref, hid_ref, feat_ref, rms_ref,
    hs, hx, fs, gv, gt, xp, pb, sb, rb, hsb, hrb, ga, fsum, pm, ar, tile, pr, cm, racc, cr, tr,
    lsem, gsend, grecv, msend, crecv, ssem, rsem, hssem, hrsem, asend, arecv, bsend, brecv,
    hsend, hrecv, psend, precv, csend, csrecv, tsend, trecv,
):
    r = lax.axis_index("row")
    c = lax.axis_index("col")
    x, yl, k = r // 4, rem(r // 2, 2), rem(r, 2)
    yh, z = c // 8, rem(c, 8)
    part = 2 * z + yh

    def row_of(dx, dy, kk):
        return rem(x + dx, 4) * 4 + rem(yl + dy, 2) * 2 + kk

    def remote(src, dst, send, recv, dev):
        return pltpu.make_async_remote_copy(
            src_ref=src, dst_ref=dst, send_sem=send, recv_sem=recv,
            device_id=dev, device_id_type=MESH,
        )

    copy_x = pltpu.make_async_copy(x_hbm, xp.at[0, k], lsem.at[0])
    copy_x.start()
    copy_g = pltpu.make_async_copy(g_hbm, gv, lsem.at[1])
    copy_g.start()
    copy_hs = pltpu.make_async_copy(hs_hbm, hs, lsem.at[2])
    copy_hs.start()
    copy_fs = pltpu.make_async_copy(fs_hbm, fs, lsem.at[3])
    copy_fs.start()

    barrier = pltpu.get_barrier_semaphore()
    diagonal = r == c
    east = (row_of(1, 0, k), c)
    west = (row_of(3, 0, k), c)
    side = (row_of(0, 1, k), c)
    mate = (row_of(0, 0, 1 - k), c)
    y_mate = (r, (1 - yh) * 8 + z)
    up = (r, yh * 8 + rem(z + 1, 8))
    down = (r, yh * 8 + rem(z + 7, 8))
    cross_up = (r, (1 - yh) * 8 + rem(z + 1, 8))
    cross_down = (r, (1 - yh) * 8 + rem(z + 7, 8))
    peers = (cross_up, cross_down, y_mate, east, west, side, up, down, mate)
    for dev in peers:
        pl.semaphore_signal(barrier, inc=1, device_id=dev, device_id_type=MESH)
    copy_x.wait()
    pl.semaphore_wait(barrier, len(peers))

    size = tokens // 4
    spans = {
        "a": pl.ds(0, tokens), "l": pl.ds(0, 2 * size), "h": pl.ds(2 * size, 2 * size),
        "l1": pl.ds(0, size), "l2": pl.ds(size, size), "h1": pl.ds(2 * size, size), "h2": pl.ds(3 * size, size),
    }
    routes = {
        "e0h": (0, 3, "h", east), "e0l": (0, 3, "l", east), "w0l": (0, 2, "l", west), "w0h": (0, 2, "h", west),
        "s0l1": (0, 1, "l1", side), "s0h1": (0, 1, "h1", side), "s0l2": (0, 1, "l2", side), "s0h2": (0, 1, "h2", side),
        "e1l1": (1, 6, "l1", east), "e1l2": (1, 6, "l2", east), "w1h1": (1, 5, "h1", west), "w1h2": (1, 5, "h2", west),
        "e3l": (3, 4, "l", east), "w2h": (2, 4, "h", west), "s2l": (2, 5, "l", side), "s3h": (3, 6, "h", side),
        "e6l": (6, 7, "l", east), "w5h": (5, 7, "h", west),
    }
    number = {name: i for i, name in enumerate(routes)}
    arrives = {(there, rows): number[name] for name, (_, there, rows, _) in routes.items()}

    def block_copy(name):
        here, there, rows, dev = routes[name]
        i = number[name]
        return remote(xp.at[here, k, spans[rows]], xp.at[there, k, spans[rows]], gsend, grecv.at[i], dev)

    def forward(*names):
        for name in names:
            block_copy(name).start()

    def wait_rows(slot, *rows):
        for one in rows:
            i = arrives[slot, one]
            ref = xp.at[slot, k, spans[one]]
            remote(ref, ref, gsend, grecv.at[i], mate).wait_recv()

    def mate_copy(slot):
        return remote(xp.at[slot, k], xp.at[slot, k], msend, crecv.at[slot], mate)

    def wait_mate(slot):
        remote(xp.at[slot, 1 - k], xp.at[slot, 1 - k], msend, crecv.at[slot], mate).wait_recv()

    forward("e0h", "w0l", "s0l1", "s0h1", "e0l", "w0h", "s0l2", "s0h2")
    mate_copy(0).start()

    def hx_copy(i):
        to = rem(c + i, 16)
        return remote(hs.at[(2 * rem(to, 8) + to // 8) // 4], hx, hsend, hrecv, (r, to))

    copy_g.wait()
    copy_fs.wait()
    copy_hs.wait()
    gt[...] = gv[...].T
    racc[...] = jnp.zeros_like(racc)

    def z_dev(sign):
        return (r, yh * 8 + rem(z + sign + 8, 8))

    def message(s, m, sign):
        return remote(sb.at[s, m], rb.at[s, m], ssem, rsem.at[s, m], z_dev(sign))

    def chunk(s, offset):
        rows = pl.ds(pl.multiple_of(rem(z + offset + 8, 8) * 64, 64), 64)
        return pb[s, rows, :]

    def put(s, m, sign, value):
        sb[s, m] = encode(value)
        message(s, m, sign).start()

    def got(s, m):
        message(s, m, 1).wait_recv()
        return decode(rb[s, m])

    def slot_offset(p):
        dy = jnp.where(jnp.logical_or(p == 1, p >= 5), 1, 0)
        one = jnp.logical_or(p == 2, p == 5)
        three = jnp.logical_or(p == 3, p == 6)
        two = jnp.logical_or(p == 4, p == 7)
        dx = jnp.where(one, 1, 0) + jnp.where(two, 2, 0) + jnp.where(three, 3, 0)
        return dx, dy

    def half_copy(s, way, q):
        to = (r, q * 8 + rem(z + 9 - 2 * way, 8))
        return remote(hsb.at[s, 2 * way + q], hrb.at[s, 2 * way + yh], hssem, hrsem.at[s, 2 * way + yh], to)

    def y_copy(s):
        return remote(hsb.at[s, 4], hrb.at[s, 4], hssem, hrsem.at[s, 4], y_mate)

    def got_half(s, i):
        remote(hsb.at[s, i], hrb.at[s, i], hssem, hrsem.at[s, i], y_mate).wait_recv()
        return decode(hrb[s, i])

    def own_rows(s, q):
        return pb[s, pl.ds(pl.multiple_of(z * 64 + q * 32, 32), 32), :]

    def a_copy(s, kk, f):
        return remote(ga.at[s, kk], ar.at[r], asend, arecv, (f, c))

    def p_copy(s, kk, f):
        return remote(pm.at[s, kk], pr.at[r], psend, precv, (f, c))

    def mine(s, kk):
        return jnp.logical_and(s == 0, k == kk)

    def step(kind, s):

        @pl.when(kind == 0)
        def _():
            wait_mate(s)
            both = jnp.concatenate([xp[s, 0], xp[s, 1]], axis=1)
            pb[s] = jnp.dot(gt[...], both, preferred_element_type=jnp.float32)
            put(s, 0, 1 - 2 * rem(s, 2), chunk(s, 4))

        @pl.when(kind == 1)
        def _():
            for way, sign in ((0, 1), (1, -1)):
                long = rem(s, 2) == way

                @pl.when(long)
                def _():
                    put(s, 1 + way, sign, chunk(s, sign * 3) + got(s, 0))

                @pl.when(not long)
                def _():
                    put(s, 1 + way, sign, chunk(s, sign * 3))

            hsb[s, 4] = encode(own_rows(s, 1 - yh))
            y_copy(s).start()

        @pl.when(kind == 2)
        def _():
            for way, sign in ((0, 1), (1, -1)):
                put(s, 3 + way, sign, chunk(s, sign * 2) + got(s, 1 + way))

        @pl.when(kind == 3)
        def _():
            for way, sign in ((0, 1), (1, -1)):
                value = chunk(s, sign) + got(s, 3 + way)
                for q in (0, 1):
                    hsb[s, 2 * way + q] = encode(value[32 * q:32 * q + 32])
                    half_copy(s, way, q).start()

        @pl.when(kind == 4)
        def _():
            g = own_rows(s, yh)
            for i in (4, 0, 1, 2, 3):
                g = g + got_half(s, i)
            squares = g * g + 1e-30
            racc[...] += squares
            dx, dy = slot_offset(s)
            for kk in (0, 1):
                ga[s, kk] = g[:, kk * 128:(kk + 1) * 128]
                fsum[s, kk] = jnp.sum(squares[:, kk * 128:(kk + 1) * 128], axis=0, keepdims=True)

                @pl.when(k == kk if s == 0 else False)
                def _():
                    ar[r] = g[:, kk * 128:(kk + 1) * 128]

                @pl.when(k != kk if s == 0 else True)
                def _():
                    a_copy(s, kk, row_of(dx, dy, kk)).start()

        @pl.when(kind == 6)
        def _():
            wait_rows(1, "l1", "h1")
            forward("e1l1", "w1h1")
            wait_rows(2, "l")
            forward("s2l")
            wait_rows(3, "h")
            forward("s3h")

        @pl.when(kind == 7)
        def _():
            wait_rows(1, "l2", "h2")
            forward("e1l2", "w1h2")
            wait_rows(3, "l")
            forward("e3l")
            wait_rows(2, "h")
            forward("w2h")
            for slot in (1, 2, 3):
                mate_copy(slot).start()

        @pl.when(kind == 10)
        def _():
            wait_rows(6, "l1", "l2")
            forward("e6l")
            wait_rows(5, "h1", "h2")
            forward("w5h")

        for slot, rows in ((4, ("l", "h")), (5, ("l",)), (6, ("h",)), (7, ("l", "h"))):
            @pl.when(kind == 8 and s == slot)
            def _():
                wait_rows(slot, *rows)
                mate_copy(slot).start()

        @pl.when(jnp.logical_and(kind == 9, diagonal) if kind == 9 else False)
        def _():
            hx[...] = hs[part // 4]
            for i in range(1, 16):
                hx_copy(i).start()

    for kind, s in PLAN:
        step(kind, s)

    @pl.when(jnp.logical_not(diagonal))
    def _():
        hx_copy(1).wait_recv()

    sums = jnp.sum(racc[...], axis=1, keepdims=True)
    lane = lax.broadcasted_iota(jnp.int32, (32, 128), 1)
    line = lax.broadcasted_iota(jnp.int32, (32, 128), 0)
    place = lane == line + rem(part, 4) * 32
    old = jnp.sum(jnp.where(place, hx[...], 0.0), axis=1, keepdims=True)
    hid = decay_rate * old + (1.0 - decay_rate) * (sums / feat_count)
    hid_row = jnp.sum(jnp.where(place, hid, 0.0), axis=0, keepdims=True)
    hid_sum = jnp.full((1, 128), jnp.sum(hid), jnp.float32)
    inverse = 1.0 / hid

    for s in range(PAIRS):
        for kk in (0, 1):
            weighted = jnp.sum(ga[s, kk] * ga[s, kk] * inverse, axis=0, keepdims=True)
            pm[s, kk] = jnp.concatenate([hid_row, fsum[s, kk], weighted, hid_sum, jnp.zeros((4, 128), jnp.float32)], axis=0)
            if s == 0:
                @pl.when(k == kk)
                def _():
                    pr[r] = pm[s, kk]

                @pl.when(k != kk)
                def _():
                    p_copy(s, kk, row_of(*slot_offset(s), kk)).start()
            else:
                p_copy(s, kk, row_of(*slot_offset(s), kk)).start()

    def left(ref, sem):
        remote(ref, ref, sem, sem, mate).wait_send()

    def came(ref, sem):
        remote(ref, ref, sem, sem, mate).wait_recv()

    left(sb, ssem)
    left(hsb, hssem)
    left(xp.at[:, 0], msend)
    left(xp.at[0:7, 0], gsend)
    left(ar.at[0:15], asend)
    came(cr.at[0:15], precv)
    totals = jnp.sum(pr[...], axis=0)
    top = lax.broadcasted_iota(jnp.int32, (8, 128), 0) == 0
    for q in range(16):
        cm[q] = jnp.where(top, pr[q], totals)
    cr[part] = cm[c]

    def c_copy(i):
        q = rem(c + i, 16)
        return remote(cm.at[q], cr.at[part], csend, csrecv, (r, q))

    for i in (8, 7, 9, 4, 12, 5, 11, 3, 13, 6, 10, 2, 14, 1, 15):
        c_copy(i).start()

    def b_copy(q):
        return remote(ar.at[q], tile.at[part], bsend, brecv, (r, q))

    came(ar.at[0:15], arecv)
    tile[part] = ar[c]
    for i in range(1, 16):
        b_copy(rem(c + i, 16)).start()
    left(cr.at[0:15], psend)

    @pl.when(diagonal)
    def _():
        left(tr.at[0:15], hsend)

    came(cr.at[0:15], csrecv)
    both = jnp.sum(cr[...], axis=0)
    feat = decay_rate * fs[...] + (1.0 - decay_rate) * (both[1:2, :] / hid_count)
    feat_ref[...] = feat
    hid_mean = both[3:4, :] / hid_count
    tr[r] = jnp.full((1, 128), jnp.sum(both[2:3, :] / feat), jnp.float32)

    def t_copy(i):
        return remote(tr.at[r], tr.at[r], tsend, trecv, (rem(r + i, 16), c))

    for i in (12, 4, 8, 13, 14, 15, 9, 10, 11, 5, 6, 7, 3, 2, 1):
        t_copy(i).start()

    eye = lax.broadcasted_iota(jnp.int32, (128, 128), 0) == lax.broadcasted_iota(jnp.int32, (128, 128), 1)
    columns = []
    for q in range(4):
        line_q = cr[4 * q, 0:1] + cr[4 * q + 1, 0:1] + cr[4 * q + 2, 0:1] + cr[4 * q + 3, 0:1]
        hid_ref[q:q + 1, :] = line_q
        columns.append(lax.rsqrt(jnp.sum(jnp.where(eye, line_q, 0.0), axis=1, keepdims=True)))

    across0 = jnp.sqrt(hid_mean / feat)
    came(tile.at[0:15], brecv)
    left(cr.at[0:15], csend)
    left(ar.at[0:15], bsend)
    came(tr.at[0:15], trecv)
    mean = hid_mean * jnp.sum(tr[...], axis=0) / (hid_count * feat_count)
    rms = jnp.sqrt(mean)
    rms_ref[...] = rms
    across = across0 / jnp.maximum(1.0, rms)
    for q in range(4):
        g = tile[4 * q:4 * q + 4].reshape(128, 128)
        upd_ref[128 * q:128 * q + 128, :] = g * columns[q] * across

    left(tr.at[0:15], tsend)


def writer(a, b, c, d, oa, ob, oc, od, sem):
    copies = [pltpu.make_async_copy(src, dst, sem.at[i]) for i, (src, dst) in enumerate(((a, oa), (b, ob), (c, oc), (d, od)))]
    for copy in copies:
        copy.start()
    for copy in copies:
        copy.wait()


def body(layer_input, grad_output, hid_state, feat_state):
    tokens = layer_input.shape[0]
    hid_count, feat_count = 8192.0, 2048.0
    vm = pl.BlockSpec(memory_space=pltpu.VMEM)
    hbm = pl.BlockSpec(memory_space=pl.ANY)
    f32, bf16 = jnp.float32, jnp.bfloat16
    dma = pltpu.SemaphoreType.DMA
    shapes = (
        jax.ShapeDtypeStruct((512, 128), f32),
        jax.ShapeDtypeStruct((4, 128), f32),
        jax.ShapeDtypeStruct((1, 128), f32),
        jax.ShapeDtypeStruct((1, 128), f32),
    )
    outs = pl.pallas_call(
        functools.partial(kernel, tokens, hid_count, feat_count),
        name="optimizer_step",
        out_shape=tuple(pltpu.VMEM(one.shape, one.dtype) for one in shapes),
        in_specs=[pl.BlockSpec(memory_space=pltpu.HBM)] * 4,
        out_specs=(vm, vm, vm, vm),
        scratch_shapes=[
            pltpu.VMEM((4, 1, 128), f32),
            pltpu.VMEM((1, 128), f32),
            pltpu.VMEM((1, 128), f32),
            pltpu.VMEM((tokens, 512), bf16),
            pltpu.VMEM((512, tokens), bf16),
            pltpu.VMEM((PAIRS, 2, tokens, 128), bf16),
            pltpu.VMEM((PAIRS, 512, 256), f32),
            pltpu.VMEM((PAIRS, 5, TILE, 128), MSG),
            pltpu.VMEM((PAIRS, 5, TILE, 128), MSG),
            pltpu.VMEM((PAIRS, 5, HALF, 128), MSG),
            pltpu.VMEM((PAIRS, 5, HALF, 128), MSG),
            pltpu.VMEM((PAIRS, 2, 32, 128), f32),
            pltpu.VMEM((PAIRS, 2, 1, 128), f32),
            pltpu.VMEM((PAIRS, 2, 8, 128), f32),
            pltpu.VMEM((16, 32, 128), f32),
            pltpu.VMEM((16, 32, 128), f32),
            pltpu.VMEM((16, 8, 128), f32),
            pltpu.VMEM((16, 8, 128), f32),
            pltpu.VMEM((32, 256), f32),
            pltpu.VMEM((16, 8, 128), f32),
            pltpu.VMEM((16, 1, 128), f32),
            dma((4,)), dma, dma((18,)), dma, dma((PAIRS,)),
            dma, dma((PAIRS, 5)), dma, dma((PAIRS, 5)), dma, dma, dma, dma,
            dma, dma, dma, dma, dma, dma, dma, dma,
        ],
        compiler_params=pltpu.CompilerParams(
            collective_id=0, has_side_effects=True, vmem_limit_bytes=62 << 20
        ),
    )(layer_input, grad_output, hid_state.reshape(4, 1, 128), feat_state.reshape(1, 128))
    update, hid, feat, rms = pl.pallas_call(
        writer,
        name="write_results",
        out_shape=shapes,
        in_specs=[vm] * 4,
        out_specs=[pl.BlockSpec(memory_space=pltpu.HBM)] * 4,
        scratch_shapes=[dma((4,))],
        compiler_params=pltpu.CompilerParams(vmem_limit_bytes=1 << 20),
    )(*outs)
    return update, hid.reshape(512), feat.reshape(128), rms[0, 0]


def solution(mesh):
    in_specs = (P("col", "row"), P("col", "row"), P("col"), P("row"))
    out_specs = (P("col", "row"), P("col"), P("row"), P())
    return jax.shard_map(body, mesh=mesh, in_specs=in_specs, out_specs=out_specs, check_vma=False)
```
